256 devices in a mesh: inst: 32 (over z, y), tp: 8 (over x, core).
Axes of the slice: x: 4, y: 4, z: 8, core: 2. Of those that a mesh axis runs over, the one named last changes fastest.
Arguments:
- caches: bfloat16 [2, 128, 512, 1024], P(None, 'inst', None, 'tp'), may hold values from -6 to 6
- queries: bfloat16 [2, 128, 8192], P(None, 'inst', 'tp'), may hold values from -140 to 140
- new_entries: bfloat16 [2, 2, 128, 1024], P(None, None, 'inst', 'tp'), may hold values from -6 to 6
- lengths: int32 [128], replicated, may hold values from 2 to 510, as said below
- targets: int32 [128], replicated, may hold values from 0 to 127, as said below
- output_weight: bfloat16 [8192, 5120], P('tp'), may hold values from -0.375 to 0.375
Outputs:
- step_one_out: bfloat16 [128, 5120], P('inst', 'tp')
- step_two_out: bfloat16 [128, 5120], P('inst', 'tp')
- caches_after: bfloat16 [2, 128, 512, 1024], P(None, 'inst', None, 'tp')
The draws below stay inside these ranges and needn't reach their ends.
Inputs may be any that keep to these rules, and one draw needn't show every extreme that they name: `lengths`: some request has exactly 510. `targets`: a permutation of the 128 slots (slot i * 4 + j is slot j of instance i); from every instance exactly 2 requests move to other instances and every other request keeps its slot; for each k the k-th leaving request (in slot order) of every instance moves the same number of instances forward along inst, cyclically; one of these two numbers is 1 and the other 16.
All inputs are finite; a program needn't handle non-finite values.
Results may differ from the reference program's by a relative error of at most 0.022.
Values may be sent and summed in bfloat16 or wider, within the bound.
No kernel may reach another device: no remote copies, remote signals or barrier semaphores. Data moves between devices by JAX's collectives and lax.ppermute only.
A program may use at most 128 MiB of HBM per device.

```python
import jax
import jax.numpy as jnp

D = 5120
HQ = 64
KVH = 8
HD = 128
REQS = 4
CAP = 512
MOVE = 2
SLOTS = 128


def draw_caches(key, part):
    key = jax.random.fold_in(key, 11)
    stored = jnp.clip(jax.random.normal(key, (2, SLOTS, CAP, KVH * HD), jnp.float32), -6.0, 6.0)
    return stored.astype(jnp.bfloat16)


def draw_queries(key, part):
    key = jax.random.fold_in(key, 12)
    drawn = 1.5 * jnp.clip(jax.random.normal(key, (2, SLOTS, HQ * HD), jnp.float32), -6.0, 6.0)
    return drawn.astype(jnp.bfloat16)


def draw_lengths(key, part):
    key = jax.random.fold_in(key, 13)
    key_scale, key_raw, key_peak = jax.random.split(key, 3)
    instances = SLOTS // REQS
    load_scale = jnp.repeat(jax.random.randint(key_scale, (instances,), 1, 5), REQS)
    raw_counts = jax.random.randint(key_raw, (SLOTS,), 0, CAP - 3)
    lengths_now = 2 + raw_counts * load_scale // 4
    peak_slot = jax.random.randint(key_peak, (), 0, SLOTS)
    return lengths_now.at[peak_slot].set(CAP - 2).astype(jnp.int32)


def draw_targets(key, part):
    key = jax.random.fold_in(key, 14)
    key_slots, key_shift = jax.random.split(key)
    instances = SLOTS // REQS
    orders = jax.vmap(lambda single: jax.random.permutation(single, REQS))(jax.random.split(key_slots, instances))
    picked = jnp.sort(orders[:, :MOVE], axis=1)
    chosen = jnp.arange(instances)[:, None] * REQS + picked
    flip = jax.random.randint(key_shift, (), 0, 2)
    base = jnp.array([1, instances // 2], dtype=jnp.int32)
    shifts = jnp.where(flip == 1, base[::-1], base)
    aligned_to = chosen[(jnp.arange(instances)[:, None] + shifts[None, :]) % instances, jnp.arange(MOVE)[None, :]]
    result = jnp.arange(SLOTS).at[chosen.reshape(-1)].set(aligned_to.reshape(-1))
    return result.astype(jnp.int32)


def block_levels(stream_key, shape, cuts, smallest, largest):
    factor_of = 1.0
    for position, parts in cuts:
        steps = jax.random.uniform(jax.random.fold_in(jax.random.fold_in(stream_key, 6), position), (parts,), jnp.float32, smallest / len(cuts), largest / len(cuts))
        factor_of = factor_of * jnp.repeat(jnp.exp(steps), shape[position] // parts).reshape((-1,) + (1,) * (len(shape) - 1 - position))
    return factor_of


def scatter_about(rng, dims, deviation, reach, cuts=(), held_as=jnp.bfloat16):
    values = deviation * jax.random.normal(rng, dims, jnp.float32)
    if cuts:
        values = values * block_levels(rng, dims, cuts, -0.22, 0.18)
    return jnp.clip(values, -reach, reach).astype(held_as)


def setup_inputs(seed: int = 0) -> dict:
    key_list = jax.random.split(jax.random.key(seed), 7)
    caches = draw_caches(jax.random.fold_in(key_list[6], 71), 0)
    queries = draw_queries(jax.random.fold_in(key_list[6], 71), 0)
    new_entries = scatter_about(key_list[2], (2, 2, SLOTS, KVH * HD), 1.0, 6.0, ((2, 32), (3, 8)))
    lengths = draw_lengths(jax.random.fold_in(key_list[6], 71), 0)
    targets = draw_targets(jax.random.fold_in(key_list[6], 71), 0)
    output_weight = scatter_about(key_list[5], (HQ * HD, D), (HQ * HD // 32) ** -0.5, 0.375, ((0, 8),))
    return {"caches": caches, "queries": queries, "new_entries": new_entries, "lengths": lengths, "targets": targets, "output_weight": output_weight}


def write_token(stored, entries, lengths_now):
    positions = jnp.arange(stored.shape[2], dtype=jnp.int32)
    at_length = positions[None, None, :, None] == lengths_now[None, :, None, None]
    return jnp.where(at_length, entries[:, :, None, :], stored)


def attend(stored, query, lengths_now):
    slot_count, capacity, features = stored.shape[1], stored.shape[2], stored.shape[3]
    kv_heads = features // HD
    group_size = query.shape[1] // features
    grouped_query = query.astype(jnp.float32).reshape(slot_count, kv_heads, group_size, HD)
    key_rows = stored[0].astype(jnp.float32).reshape(slot_count, capacity, kv_heads, HD)
    value_rows = stored[1].astype(jnp.float32).reshape(slot_count, capacity, kv_heads, HD)
    scores = jnp.einsum("skgd,sckd->skgc", grouped_query, key_rows) * (HD ** -0.5)
    visible = jnp.arange(capacity, dtype=jnp.int32)[None, :] <= lengths_now[:, None]
    scores = jnp.where(visible[:, None, None, :], scores, -jnp.inf)
    row_max = jnp.max(scores, axis=-1, keepdims=True)
    weights = jnp.exp(scores - row_max)
    weights_bf = (weights / jnp.sum(weights, axis=-1, keepdims=True)).astype(jnp.bfloat16)
    weighted = jnp.einsum("skgc,sckd->skgd", weights_bf.astype(jnp.float32), value_rows)
    return weighted.reshape(slot_count, kv_heads * group_size * HD).astype(jnp.bfloat16)


def reference(caches, queries, new_entries, lengths, targets, output_weight):
    caches_one = write_token(caches, new_entries[0], lengths)
    att_one = attend(caches_one, queries[0], lengths)
    step_one_out = jnp.dot(att_one, output_weight, preferred_element_type=jnp.float32).astype(jnp.bfloat16)
    everyone = jnp.arange(targets.shape[0], dtype=jnp.int32)
    source = jnp.zeros_like(targets).at[targets].set(everyone)
    moved_caches = jnp.take(caches_one, source, axis=1)
    moved_query = jnp.take(queries[1], source, axis=0)
    moved_new = jnp.take(new_entries[1], source, axis=1)
    lengths_two = jnp.take(lengths, source) + 1
    caches_after = write_token(moved_caches, moved_new, lengths_two)
    att_two = attend(caches_after, moved_query, lengths_two)
    step_two_out = jnp.dot(att_two, output_weight, preferred_element_type=jnp.float32).astype(jnp.bfloat16)
    return step_one_out, step_two_out, caches_after
```

```python
import functools

import jax
import jax.numpy as jnp
from jax import lax
from jax.experimental import pallas as pl
from jax.experimental.pallas import tpu as pltpu
from jax.sharding import PartitionSpec as P

HD = 128
REQS = 4
CAP = 512
TILE = 16


def bcast_rows(row, rows):
    return jnp.broadcast_to(row, (rows, row.shape[-1]))


def write_row(ref, lead, position, row):
    base = pl.multiple_of((position // TILE) * TILE, TILE)
    window = ref[lead + (pl.ds(base, TILE), slice(None))]
    at = lax.broadcasted_iota(jnp.int32, window.shape, 0) == position - base
    ref[lead + (pl.ds(base, TILE), slice(None))] = jnp.where(at, bcast_rows(row, TILE), window)


def pick_row(rows, slot):
    at = lax.broadcasted_iota(jnp.int32, rows.shape, 0) == slot
    return jnp.sum(jnp.where(at, rows.astype(jnp.float32), 0.0), axis=0, keepdims=True).astype(rows.dtype)


def find_leaver(targets_ref, source_inst, target_inst):
    slot = jnp.int32(0)
    place = jnp.int32(0)
    for j in range(REQS):
        t = targets_ref[source_inst * REQS + j]
        hit = t // REQS == target_inst
        slot = jnp.where(hit, j, slot)
        place = jnp.where(hit, t % REQS, place)
    return slot, place


def prep_kernel(shifts, groups, targets_ref, lengths_ref, new_ref, caches_ref, *rest):
    outs, sems = rest[:-1], rest[-1]
    me = lax.axis_index("inst")
    slots = []
    for n, shift in enumerate(shifts):
        slot, _ = find_leaver(targets_ref, me, lax.rem(me + shift, groups))
        slots.append(slot)
        for kv in range(2):
            pltpu.make_async_copy(caches_ref.at[kv, slot], outs[n].at[kv], sems.at[n, kv]).start()
    for n, shift in enumerate(shifts):
        slot = slots[n]
        length = lengths_ref[me * REQS + slot]
        for kv in range(2):
            pltpu.make_async_copy(caches_ref.at[kv, slot], outs[n].at[kv], sems.at[n, kv]).wait()
            for step in range(2):
                write_row(outs[n], (kv,), length + step, pick_row(new_ref[step, kv], slot))


def attend_kernel(shifts, groups, targets_ref, lengths_ref, queries_ref, new_ref, caches_ref,
                  att_ref, after_ref, *rest):
    pays = rest[: len(shifts)]
    stored, att, in_sems, out_sems = rest[len(shifts):]
    me = lax.axis_index("inst")

    def load(s, kv):
        return pltpu.make_async_copy(caches_ref.at[kv, s], stored.at[kv, s], in_sems.at[kv, s])

    def save(s, kv):
        return pltpu.make_async_copy(stored.at[kv, s], after_ref.at[kv, s], out_sems.at[kv, s])

    for s in range(REQS):
        for kv in range(2):
            load(s, kv).start()
    for s in range(REQS):
        length = lengths_ref[me * REQS + s]
        for kv in range(2):
            load(s, kv).wait()
            for step in range(2):
                write_row(stored, (kv, s), length + step, new_ref[step, kv, s:s + 1, :])
            save(s, kv).start()
        query = jnp.concatenate(
            [queries_ref[0, s], queries_ref[1, s]], axis=0
        )
        scores = lax.dot_general(
            query, stored[0, s], (((1,), (1,)), ((), ())), preferred_element_type=jnp.float32
        ) * HD ** (-0.5)
        live = length + (lax.broadcasted_iota(jnp.int32, scores.shape, 0) >= 8).astype(jnp.int32)
        visible = lax.broadcasted_iota(jnp.int32, scores.shape, 1) <= live
        scores = jnp.where(visible, scores, -jnp.inf)
        weights = jnp.exp(scores - jnp.max(scores, axis=-1, keepdims=True))
        weights = weights / jnp.sum(weights, axis=-1, keepdims=True)
        out = jnp.dot(weights.astype(jnp.bfloat16), stored[1, s], preferred_element_type=jnp.float32)
        out = out.astype(jnp.bfloat16).astype(jnp.float32)
        att[pl.ds(s * 8, 8), :] = out[:8]
        att[pl.ds((REQS + s) * 8, 8), :] = out[8:]
    att_ref[...] = att[...]
    for n, shift in enumerate(shifts):
        slot, _ = find_leaver(targets_ref, me, lax.rem(me + shift, groups))
        row = att[pl.ds(pl.multiple_of((REQS + slot) * 8, 8), 8), :]
        pays[n][...] = jnp.concatenate([row, row], axis=0).astype(jnp.bfloat16)
    for s in range(REQS):
        for kv in range(2):
            save(s, kv).wait()


def project_kernel(shifts, groups, parts, targets_ref, att_ref, *rest):
    pays = rest[: len(shifts)]
    weight_ref, out_ref, att, lhs, weight, sems = rest[len(shifts):]
    me = lax.axis_index("inst")
    width = out_ref.shape[-1]

    def load(p):
        cols = pl.ds(p * width, width)
        return pltpu.make_async_copy(weight_ref.at[:, cols], weight.at[:, cols], sems.at[p])

    for p in range(parts):
        load(p).start()
    att[...] = att_ref[...]
    for n, shift in enumerate(shifts):
        _, place = find_leaver(targets_ref, lax.rem(me + groups - shift, groups), me)
        att[pl.ds(pl.multiple_of((REQS + place) * 8, 8), 8), :] = pays[n][...].astype(jnp.float32)[:8]
    for h in range(8):
        lhs[:, h * HD:(h + 1) * HD] = att[pl.ds(h, 2 * REQS, stride=8), :].astype(jnp.bfloat16)
    for p in range(parts):
        load(p).wait()
        out_ref[p] = jnp.dot(
            lhs[...], weight[:, p * width:(p + 1) * width], preferred_element_type=jnp.float32
        ).astype(jnp.bfloat16)


def finish_kernel(shifts, groups, targets_ref, parts_ref, *rest):
    moved = rest[: len(shifts)]
    _, one_ref, two_ref, after_ref, sems = rest[len(shifts):]
    me = lax.axis_index("inst")
    copies = []
    for n, shift in enumerate(shifts):
        _, place = find_leaver(targets_ref, lax.rem(me + groups - shift, groups), me)
        copies.append(pltpu.make_async_copy(moved[n], after_ref.at[:, place], sems.at[n]))
        copies[-1].start()
    total = jnp.sum(parts_ref[...].astype(jnp.float32), axis=0)
    one_ref[...] = total[:REQS].astype(jnp.bfloat16)
    two_ref[...] = total[REQS:].astype(jnp.bfloat16)
    for copy in copies:
        copy.wait()


VM = pl.BlockSpec(memory_space=pltpu.VMEM)
SM = pl.BlockSpec(memory_space=pltpu.SMEM)
ANY = pl.BlockSpec(memory_space=pl.ANY)
BF = jnp.bfloat16


def shape(dims, kind=BF):
    return jax.ShapeDtypeStruct(dims, kind)


def on_device(caches, queries, new_entries, lengths, targets, output_weight):
    groups = lax.axis_size("inst")
    parts = lax.axis_size("tp")
    shifts = (groups // 2, 1)
    width = output_weight.shape[1] // parts
    perms = [[(i, (i + s) % groups) for i in range(groups)] for s in shifts]

    sent = pl.pallas_call(
        functools.partial(prep_kernel, shifts, groups),
        out_shape=[shape((2, CAP, HD))] * 2,
        in_specs=[SM, SM, VM, ANY],
        out_specs=[VM, VM],
        scratch_shapes=[pltpu.SemaphoreType.DMA((2, 2))],
        name="prep",
    )(targets, lengths, new_entries, caches)
    moved = [lax.ppermute(x, "inst", perm) for x, perm in zip(sent, perms)]

    heads = queries.reshape(2, REQS, 8, HD)
    att, after, *pays = pl.pallas_call(
        functools.partial(attend_kernel, shifts, groups),
        out_shape=[shape((64, HD), jnp.float32), shape(caches.shape)] + [shape((16, HD))] * 2,
        in_specs=[SM, SM, VM, VM, ANY],
        out_specs=[VM, ANY, VM, VM],
        scratch_shapes=[
            pltpu.VMEM(caches.shape, BF),
            pltpu.VMEM((64, HD), jnp.float32),
            pltpu.SemaphoreType.DMA((2, REQS)),
            pltpu.SemaphoreType.DMA((2, REQS)),
        ],
        name="attend",
    )(targets, lengths, heads, new_entries, caches)
    pays = [lax.ppermute(x, "inst", perm) for x, perm in zip(pays, perms)]

    partial = pl.pallas_call(
        functools.partial(project_kernel, shifts, groups, parts),
        out_shape=shape((parts, 2 * REQS, width)),
        in_specs=[SM, VM, VM, VM, ANY],
        out_specs=VM,
        scratch_shapes=[
            pltpu.VMEM((64, HD), jnp.float32),
            pltpu.VMEM((2 * REQS, 8 * HD), BF),
            pltpu.VMEM(output_weight.shape, BF),
            pltpu.SemaphoreType.DMA((parts,)),
        ],
        compiler_params=pltpu.CompilerParams(vmem_limit_bytes=24 << 20),
        name="project",
    )(targets, att, *pays, output_weight)
    shares = lax.all_to_all(partial, "tp", 0, 0)

    one, two, after = pl.pallas_call(
        functools.partial(finish_kernel, shifts, groups),
        out_shape=[shape((REQS, width)), shape((REQS, width)), shape(caches.shape)],
        in_specs=[SM, VM, ANY, ANY, ANY],
        out_specs=[VM, VM, ANY],
        input_output_aliases={4: 2},
        scratch_shapes=[pltpu.SemaphoreType.DMA((2,))],
        name="finish",
    )(targets, shares, *moved, after)
    return one, two, after


def solution(mesh):
    placed = (
        P(None, "inst", None, "tp"),
        P(None, "inst", "tp"),
        P(None, None, "inst", "tp"),
        P(),
        P(),
        P("tp", None),
    )
    return jax.shard_map(
        on_device,
        mesh=mesh,
        in_specs=placed,
        out_specs=(P("inst", "tp"), P("inst", "tp"), P(None, "inst", None, "tp")),
        check_vma=False,
    )
```

```python
import functools

import jax
import jax.numpy as jnp
from jax import lax
from jax.experimental import pallas as pl
from jax.experimental.pallas import tpu as pltpu
from jax.sharding import PartitionSpec as P

HD = 128
REQS = 4
CAP = 512
TILE = 16


def bcast_rows(row, rows):
    return jnp.broadcast_to(row, (rows, row.shape[-1]))


def write_row(ref, lead, position, row):
    base = pl.multiple_of((position // TILE) * TILE, TILE)
    window = ref[lead + (pl.ds(base, TILE), slice(None))]
    at = lax.broadcasted_iota(jnp.int32, window.shape, 0) == position - base
    ref[lead + (pl.ds(base, TILE), slice(None))] = jnp.where(at, bcast_rows(row, TILE), window)


def pick_row(rows, slot):
    at = lax.broadcasted_iota(jnp.int32, rows.shape, 0) == slot
    return jnp.sum(jnp.where(at, rows.astype(jnp.float32), 0.0), axis=0, keepdims=True).astype(rows.dtype)


def find_leaver(targets_ref, source_inst, target_inst):
    slot = jnp.int32(0)
    place = jnp.int32(0)
    for j in range(REQS):
        t = targets_ref[source_inst * REQS + j]
        hit = t // REQS == target_inst
        slot = jnp.where(hit, j, slot)
        place = jnp.where(hit, t % REQS, place)
    return slot, place


def step_two_rows(targets_ref, me, shifts, groups):
    rows = []
    rank = jnp.int32(REQS)
    for j in range(REQS):
        inst = targets_ref[me * REQS + j] // REQS
        row = rank
        for n, shift in enumerate(shifts):
            row = jnp.where(inst == lax.rem(me + shift, groups), 2 * REQS - len(shifts) + n, row)
        rows.append(row)
        rank = rank + (inst == me).astype(jnp.int32)
    return rows


def start_all(pairs, sems):
    copies = [pltpu.make_async_copy(a, b, sems.at[n]) for n, (a, b) in enumerate(pairs)]
    for copy in copies:
        copy.start()
    return copies


def wait_all(copies):
    for copy in copies:
        copy.wait()


def prep_kernel(shifts, groups, targets_hbm, lengths_hbm, new_hbm, caches_hbm, *rest):
    outs = rest[:len(shifts)]
    targets, lengths, new, stored, small_sems, sems = rest[len(shifts):]
    me = lax.axis_index("inst")
    smalls = start_all([(targets_hbm, targets), (lengths_hbm, lengths), (new_hbm, new)], small_sems)
    bigs = start_all([(caches_hbm.at[:, s], stored.at[:, s]) for s in range(REQS)], sems)
    wait_all(smalls)
    wait_all(bigs)
    for n, shift in enumerate(shifts):
        slot, _ = find_leaver(targets, me, lax.rem(me + shift, groups))
        length = lengths[me * REQS + slot]
        for kv in range(2):
            outs[n][kv] = stored[kv, slot]
            for step in range(2):
                write_row(outs[n], (kv,), length + step, pick_row(new[step, kv], slot))


def step_kernel(shifts, groups, parts, targets_hbm, lengths_hbm, queries_hbm, new_hbm, caches_ref, weight_ref,
                out_ref, after_ref, targets_ref, lengths_ref, queries_ref, new_ref, stored, weight, query,
                att, lhs, small_sems, in_sems, out_sems, w_sems):
    me = lax.axis_index("inst")
    width = out_ref.shape[-1]

    def load(s, kv):
        return pltpu.make_async_copy(caches_ref.at[kv, s], stored.at[kv, s], in_sems.at[kv, s])

    def save(s, kv):
        return pltpu.make_async_copy(stored.at[kv, s], after_ref.at[kv, s], out_sems.at[kv, s])

    def load_weight(p):
        cols = pl.ds(p * width, width)
        return pltpu.make_async_copy(weight_ref.at[:, cols], weight.at[:, cols], w_sems.at[p])

    smalls = start_all(
        [(queries_hbm, queries_ref), (new_hbm, new_ref), (lengths_hbm, lengths_ref), (targets_hbm, targets_ref)],
        small_sems,
    )
    for kv in range(2):
        for s in range(REQS):
            load(s, kv).start()
    for p in range(parts):
        load_weight(p).start()
    wait_all(smalls)
    for step in range(2):
        for h in range(8):
            rows = queries_ref[step, :, h * HD:(h + 1) * HD].astype(jnp.float32)
            query[pl.ds(step * 8 + h, REQS, stride=16), :] = rows
    for kv in range(2):
        for s in range(REQS):
            load(s, kv).wait()
            for step in range(2):
                write_row(stored, (kv, s), lengths_ref[me * REQS + s] + step, new_ref[step, kv, s:s + 1, :])
            save(s, kv).start()
    probs = []
    for s in range(REQS):
        scores = lax.dot_general(
            query[s * 16:(s + 1) * 16, :].astype(BF), stored[0, s], (((1,), (1,)), ((), ())),
            preferred_element_type=jnp.float32,
        ) * HD ** (-0.5)
        live = lengths_ref[me * REQS + s] + (
            lax.broadcasted_iota(jnp.int32, scores.shape, 0) >= 8
        ).astype(jnp.int32)
        visible = lax.broadcasted_iota(jnp.int32, scores.shape, 1) <= live
        scores = jnp.where(visible, scores, -jnp.inf)
        weights = jnp.exp(scores - jnp.max(scores, axis=-1, keepdims=True))
        probs.append((weights / jnp.sum(weights, axis=-1, keepdims=True)).astype(BF))
    rows_two = step_two_rows(targets_ref, me, shifts, groups)
    for s in range(REQS):
        out = jnp.dot(probs[s], stored[1, s], preferred_element_type=jnp.float32)
        att[pl.ds(s * 8, 8), :] = out[:8]
        att[pl.ds(pl.multiple_of(rows_two[s] * 8, 8), 8), :] = out[8:]
    for h in range(8):
        lhs[:, h * HD:(h + 1) * HD] = att[pl.ds(h, 2 * REQS, stride=8), :].astype(BF)
    for p in range(parts):
        load_weight(p).wait()
        out_ref[p] = jnp.dot(
            lhs[...], weight[:, p * width:(p + 1) * width], preferred_element_type=jnp.float32
        ).astype(BF)
    for kv in range(2):
        for s in range(REQS):
            save(s, kv).wait()


def sum_kernel(shares_ref, one_ref, stay_ref, *pays):
    total = jnp.sum(shares_ref[...].astype(jnp.float32), axis=0)
    one_ref[...] = total[:REQS].astype(BF)
    stay_ref[...] = total
    for n, pay in enumerate(pays):
        row = 2 * REQS - len(pays) + n
        pay[...] = bcast_rows(total[row:row + 1], pay.shape[0]).astype(BF)


def finish_kernel(shifts, groups, targets_hbm, stay_ref, *rest):
    many = len(shifts)
    pays, moved = rest[:many], rest[many:2 * many]
    _, two_ref, after_ref, targets_ref, sem, sems = rest[2 * many:]
    me = lax.axis_index("inst")
    copy = pltpu.make_async_copy(targets_hbm, targets_ref, sem)
    copy.start()
    copy.wait()
    places = []
    copies = []
    for n, shift in enumerate(shifts):
        _, place = find_leaver(targets_ref, lax.rem(me + groups - shift, groups), me)
        places.append(place)
        copies.append(pltpu.make_async_copy(moved[n], after_ref.at[:, place], sems.at[n]))
        copies[-1].start()
    rows_two = step_two_rows(targets_ref, me, shifts, groups)
    at = lax.broadcasted_iota(jnp.int32, two_ref.shape, 0)
    out = jnp.zeros(two_ref.shape, jnp.float32)
    for r in range(REQS, 2 * REQS - many):
        for s in range(REQS):
            out = jnp.where(
                (at == s) & (rows_two[s] == r), bcast_rows(stay_ref[r:r + 1, :], REQS), out
            )
    for n in range(many):
        row = pays[n][...].astype(jnp.float32)[:1]
        out = jnp.where(at == places[n], bcast_rows(row, REQS), out)
    two_ref[...] = out.astype(BF)
    for copy in copies:
        copy.wait()


VM = pl.BlockSpec(memory_space=pltpu.VMEM)
BF = jnp.bfloat16


def shape(dims, kind=BF):
    return jax.ShapeDtypeStruct(dims, kind)
HBM = pl.BlockSpec(memory_space=pltpu.HBM)


def limit(mib):
    return pltpu.CompilerParams(vmem_limit_bytes=mib << 20)


def on_device(caches, queries, new_entries, lengths, targets, output_weight):
    groups = lax.axis_size("inst")
    parts = lax.axis_size("tp")
    shifts = (groups // 2, 1)
    many = len(shifts)
    width = output_weight.shape[1] // parts
    perms = [[(i, (i + s) % groups) for i in range(groups)] for s in shifts]

    caches, queries, new_entries, lengths, targets, output_weight = [
        pltpu.with_memory_space_constraint(x, pltpu.HBM)
        for x in (caches, queries, new_entries, lengths, targets, output_weight)
    ]
    smem = pltpu.SMEM(targets.shape, jnp.int32)
    sent = pl.pallas_call(
        functools.partial(prep_kernel, shifts, groups),
        out_shape=[shape((2, CAP, HD))] * many,
        in_specs=[HBM] * 4,
        out_specs=[VM] * many,
        scratch_shapes=[
            smem,
            smem,
            pltpu.VMEM(new_entries.shape, BF),
            pltpu.VMEM(caches.shape, BF),
            pltpu.SemaphoreType.DMA((3,)),
            pltpu.SemaphoreType.DMA((REQS,)),
        ],
        compiler_params=limit(4),
        name="prep",
    )(targets, lengths, new_entries, caches)
    moved = [lax.ppermute(x, "inst", perm) for x, perm in zip(sent, perms)]

    partial, after = pl.pallas_call(
        functools.partial(step_kernel, shifts, groups, parts),
        out_shape=[shape((parts, 2 * REQS, width)), shape(caches.shape)],
        in_specs=[HBM] * 6,
        out_specs=[VM, HBM],
        scratch_shapes=[
            smem,
            smem,
            pltpu.VMEM(queries.shape, BF),
            pltpu.VMEM(new_entries.shape, BF),
            pltpu.VMEM(caches.shape, BF),
            pltpu.VMEM(output_weight.shape, BF),
            pltpu.VMEM((16 * REQS, HD), jnp.float32),
            pltpu.VMEM((16 * REQS, HD), jnp.float32),
            pltpu.VMEM((2 * REQS, 8 * HD), BF),
            pltpu.SemaphoreType.DMA((4,)),
            pltpu.SemaphoreType.DMA((2, REQS)),
            pltpu.SemaphoreType.DMA((2, REQS)),
            pltpu.SemaphoreType.DMA((parts,)),
        ],
        compiler_params=limit(20),
        name="step",
    )(targets, lengths, queries, new_entries, caches, output_weight)
    shares = lax.all_to_all(partial, "tp", 0, 0)

    one, stay, *pays = pl.pallas_call(
        sum_kernel,
        out_shape=[shape((REQS, width)), shape((2 * REQS, width), jnp.float32)] + [shape((8, width))] * many,
        in_specs=[VM],
        out_specs=[VM] * (2 + many),
        compiler_params=limit(4),
        name="sum",
    )(shares)
    pays = [lax.ppermute(x, "inst", perm) for x, perm in zip(pays, perms)]

    two, after = pl.pallas_call(
        functools.partial(finish_kernel, shifts, groups),
        out_shape=[shape((REQS, width)), shape(caches.shape)],
        in_specs=[HBM, VM] + [VM] * many + [VM] * many + [HBM],
        out_specs=[VM, HBM],
        input_output_aliases={2 + 2 * many: 1},
        scratch_shapes=[smem, pltpu.SemaphoreType.DMA, pltpu.SemaphoreType.DMA((many,))],
        compiler_params=limit(4),
        name="finish",
    )(targets, stay, *pays, *moved, after)
    return one, two, after


def solution(mesh):
    placed = (
        P(None, "inst", None, "tp"),
        P(None, "inst", "tp"),
        P(None, None, "inst", "tp"),
        P(),
        P(),
        P("tp", None),
    )
    return jax.shard_map(
        on_device,
        mesh=mesh,
        in_specs=placed,
        out_specs=(P("inst", "tp"), P("inst", "tp"), P(None, "inst", None, "tp")),
        check_vma=False,
    )
```

```python
import functools

import jax
import jax.numpy as jnp
from jax import lax
from jax.experimental import pallas as pl
from jax.experimental.pallas import tpu as pltpu
from jax.sharding import PartitionSpec as P

HD = 128
REQS = 4
CAP = 512
TILE = 16
PAY_ROWS = (16, 256)


def bcast_rows(row, rows):
    return jnp.broadcast_to(row, (rows, row.shape[-1]))


def write_row(ref, lead, position, row):
    base = pl.multiple_of((position // TILE) * TILE, TILE)
    window = ref[lead + (pl.ds(base, TILE), slice(None))]
    at = lax.broadcasted_iota(jnp.int32, window.shape, 0) == position - base
    ref[lead + (pl.ds(base, TILE), slice(None))] = jnp.where(at, bcast_rows(row, TILE), window)


def pick_row(rows, slot):
    at = lax.broadcasted_iota(jnp.int32, rows.shape, 0) == slot
    return jnp.sum(jnp.where(at, rows.astype(jnp.float32), 0.0), axis=0, keepdims=True).astype(rows.dtype)


def find_leaver(targets_ref, source_inst, target_inst):
    slot = jnp.int32(0)
    place = jnp.int32(0)
    for j in range(REQS):
        t = targets_ref[source_inst * REQS + j]
        hit = t // REQS == target_inst
        slot = jnp.where(hit, j, slot)
        place = jnp.where(hit, t % REQS, place)
    return slot, place


def attend_kernel(shifts, groups, targets_hbm, lengths_hbm, queries_hbm, new_hbm, caches_hbm, *rest):
    many = len(shifts)
    whole, halves, pays = rest[0], rest[1:3], rest[3:3 + many]
    (att, after_hbm, targets, lengths, queries, new, stored, query, small_sems, in_sems,
     out_sems) = rest[3 + many:]
    me = lax.axis_index("inst")
    smalls = [
        pltpu.make_async_copy(source, target, small_sems.at[n])
        for n, (source, target) in enumerate(
            [(lengths_hbm, lengths), (new_hbm, new), (targets_hbm, targets), (queries_hbm, queries)]
        )
    ]

    def load(s, kv):
        return pltpu.make_async_copy(caches_hbm.at[kv, s], stored.at[kv, s], in_sems.at[kv, s])

    def save(s, kv):
        return pltpu.make_async_copy(stored.at[kv, s], after_hbm.at[kv, s], out_sems.at[kv, s])

    for copy in smalls:
        copy.start()
    for kv in range(2):
        for s in range(REQS):
            load(s, kv).start()
    for copy in smalls:
        copy.wait()
    for step in range(2):
        for h in range(8):
            rows = queries[step, :, h * HD:(h + 1) * HD].astype(jnp.float32)
            query[pl.ds(step * 8 + h, REQS, stride=16), :] = rows
    for kv in range(2):
        for s in range(REQS):
            load(s, kv).wait()
            for step in range(2):
                write_row(stored, (kv, s), lengths[me * REQS + s] + step, new[step, kv, s:s + 1, :])
            save(s, kv).start()
    probs = []
    for s in range(REQS):
        scores = lax.dot_general(
            query[s * 16:(s + 1) * 16, :].astype(BF), stored[0, s], (((1,), (1,)), ((), ())),
            preferred_element_type=jnp.float32,
        ) * HD ** (-0.5)
        live = lengths[me * REQS + s] + (
            lax.broadcasted_iota(jnp.int32, scores.shape, 0) >= 8
        ).astype(jnp.int32)
        visible = lax.broadcasted_iota(jnp.int32, scores.shape, 1) <= live
        scores = jnp.where(visible, scores, -jnp.inf)
        weights = jnp.exp(scores - jnp.max(scores, axis=-1, keepdims=True))
        probs.append((weights / jnp.sum(weights, axis=-1, keepdims=True)).astype(BF))
    for s in range(REQS):
        out = jnp.dot(probs[s], stored[1, s], preferred_element_type=jnp.float32)
        att[s * 8:(s + 1) * 8, :] = out[:8]
        att[(REQS + s) * 8:(REQS + s + 1) * 8, :] = out[8:]
    for n, shift in enumerate(shifts):
        slot, _ = find_leaver(targets, me, lax.rem(me + shift, groups))
        row = att[pl.ds(pl.multiple_of((REQS + slot) * 8, 8), 8), :]
        pays[n][...] = jnp.concatenate([row] * (pays[n].shape[0] // 8), axis=0).astype(BF)
        for kv in range(2):
            if n == 0:
                whole[kv] = stored[kv, slot]
            else:
                halves[kv][...] = stored[kv, slot]
    for kv in range(2):
        for s in range(REQS):
            save(s, kv).wait()


def project_kernel(shifts, groups, parts, targets_hbm, att_ref, *rest):
    many = len(shifts)
    pays = rest[:many][::-1]
    weight_ref, out_ref, targets, att, lhs, *buffers, sem = rest[many:]
    me = lax.axis_index("inst")
    width = out_ref.shape[-1]
    if buffers:
        weight, w_sems = buffers

        def load_weight(p):
            cols = pl.ds(p * width, width)
            return pltpu.make_async_copy(weight_ref.at[:, cols], weight.at[:, cols], w_sems.at[p])

    copy = pltpu.make_async_copy(targets_hbm, targets, sem)
    copy.start()
    if buffers:
        for p in range(parts):
            load_weight(p).start()
    else:
        weight = weight_ref
    att[...] = att_ref[...]
    copy.wait()
    for n, shift in enumerate(shifts):
        _, place = find_leaver(targets, lax.rem(me + groups - shift, groups), me)
        att[pl.ds(pl.multiple_of((REQS + place) * 8, 8), 8), :] = pays[n][:16, :].astype(jnp.float32)[:8]
    for h in range(8):
        lhs[:, h * HD:(h + 1) * HD] = att[pl.ds(h, 2 * REQS, stride=8), :].astype(BF)
    for p in range(parts):
        if buffers:
            load_weight(p).wait()
        out_ref[p] = jnp.dot(
            lhs[...], weight[:, p * width:(p + 1) * width], preferred_element_type=jnp.float32
        ).astype(BF)


def sum_kernel(shares_ref, one_ref, two_ref):
    total = jnp.sum(shares_ref[...].astype(jnp.float32), axis=0)
    one_ref[...] = total[:REQS].astype(BF)
    two_ref[...] = total[REQS:].astype(BF)


def place_kernel(shifts, groups, targets_hbm, *rest):
    moved = rest[:len(shifts)]
    _, after_hbm, targets, sem, sems = rest[len(shifts):]
    me = lax.axis_index("inst")
    copy = pltpu.make_async_copy(targets_hbm, targets, sem)
    copy.start()
    copy.wait()
    copies = []
    for n, (shift, part) in enumerate(shifts):
        _, place = find_leaver(targets, lax.rem(me + groups - shift, groups), me)
        target = after_hbm.at[:, place] if part is None else after_hbm.at[part, place]
        copies.append(pltpu.make_async_copy(moved[n], target, sems.at[n]))
        copies[-1].start()
    for copy in copies:
        copy.wait()


VM = pl.BlockSpec(memory_space=pltpu.VMEM)
BF = jnp.bfloat16


def shape(dims, kind=BF):
    return jax.ShapeDtypeStruct(dims, kind)
HBM = pl.BlockSpec(memory_space=pltpu.HBM)


def limit(mib):
    return pltpu.CompilerParams(vmem_limit_bytes=mib << 20)


def on_device(caches, queries, new_entries, lengths, targets, output_weight):
    groups = lax.axis_size("inst")
    parts = lax.axis_size("tp")
    shifts = (groups // 2, 1)
    many = len(shifts)
    width = output_weight.shape[1] // parts
    perms = [[(i, (i + s) % groups) for i in range(groups)] for s in shifts]
    moves = lambda arrays: [lax.ppermute(x, "inst", perm) for x, perm in zip(arrays, perms)]

    caches, queries, new_entries, lengths, targets = [
        pltpu.with_memory_space_constraint(x, pltpu.HBM)
        for x in (caches, queries, new_entries, lengths, targets)
    ]
    *packs, att, after = pl.pallas_call(
        functools.partial(attend_kernel, shifts, groups),
        out_shape=[shape((2, CAP, HD))] + [shape((CAP, HD))] * 2 + [shape((rows, HD)) for rows in PAY_ROWS]
        + [shape((16 * REQS, HD), jnp.float32), shape(caches.shape)],
        in_specs=[HBM] * 5,
        out_specs=[VM] * (4 + many) + [HBM],
        scratch_shapes=[
            pltpu.SMEM(targets.shape, jnp.int32),
            pltpu.SMEM(lengths.shape, jnp.int32),
            pltpu.VMEM(queries.shape, BF),
            pltpu.VMEM(new_entries.shape, BF),
            pltpu.VMEM(caches.shape, BF),
            pltpu.VMEM((16 * REQS, HD), jnp.float32),
            pltpu.SemaphoreType.DMA((4,)),
            pltpu.SemaphoreType.DMA((2, REQS)),
            pltpu.SemaphoreType.DMA((2, REQS)),
        ],
        compiler_params=limit(6),
        cost_estimate=pl.CostEstimate(flops=10000000000, bytes_accessed=10**6, transcendentals=0),
        name="attend",
    )(targets, lengths, queries, new_entries, caches)
    pays = moves(packs[3:])
    whole, keys, values = [lax.ppermute(x, "inst", perms[n]) for x, n in zip(packs[:3], (0, 1, 1))]

    partial = pl.pallas_call(
        functools.partial(project_kernel, shifts, groups, parts),
        out_shape=shape((parts, 2 * REQS, width)),
        in_specs=[HBM] + [VM] * (1 + many) + [VM],
        out_specs=VM,
        scratch_shapes=[
            pltpu.SMEM(targets.shape, jnp.int32),
            pltpu.VMEM((16 * REQS, HD), jnp.float32),
            pltpu.VMEM((2 * REQS, 8 * HD), BF),
            pltpu.SemaphoreType.DMA,
        ],
        compiler_params=limit(20),
        cost_estimate=pl.CostEstimate(flops=1000000000, bytes_accessed=10**6, transcendentals=0),
        name="project",
    )(targets, att, *pays[::-1], output_weight)
    shares = lax.all_to_all(partial, "tp", 0, 0)

    one, two = pl.pallas_call(
        sum_kernel,
        out_shape=[shape((REQS, width))] * 2,
        in_specs=[VM],
        out_specs=[VM] * 2,
        compiler_params=limit(4),
        name="sum",
    )(shares)

    def place(plan, moved, after, hint):
        return pl.pallas_call(
            functools.partial(place_kernel, plan, groups),
            out_shape=shape(caches.shape),
            in_specs=[HBM] + [VM] * len(plan) + [HBM],
            out_specs=HBM,
            input_output_aliases={1 + len(plan): 0},
            scratch_shapes=[
                pltpu.SMEM(targets.shape, jnp.int32),
                pltpu.SemaphoreType.DMA,
                pltpu.SemaphoreType.DMA((len(plan),)),
            ],
            compiler_params=limit(4),
            cost_estimate=hint,
            name="place",
        )(targets, *moved, after)

    hint = pl.CostEstimate(flops=2000000000, bytes_accessed=10**6, transcendentals=0)
    after = place([(1, 0)], [keys], after, hint)
    after = place([(1, 1), (groups // 2, None)], [values, whole], after, None)
    return one, two, after


def solution(mesh):
    placed = (
        P(None, "inst", None, "tp"),
        P(None, "inst", "tp"),
        P(None, None, "inst", "tp"),
        P(),
        P(),
        P("tp", None),
    )
    return jax.shard_map(
        on_device,
        mesh=mesh,
        in_specs=placed,
        out_specs=(P("inst", "tp"), P("inst", "tp"), P(None, "inst", None, "tp")),
        check_vma=False,
    )
```

```python
import functools

import jax
import jax.numpy as jnp
from jax import lax
from jax.experimental import pallas as pl
from jax.experimental.pallas import tpu as pltpu
from jax.sharding import PartitionSpec as P

HD = 128
REQS = 4
CAP = 512
TILE = 16
FAR = 64
NEAR = 128


def bcast_rows(row, rows):
    return jnp.broadcast_to(row, (rows, row.shape[-1]))


def write_row(ref, lead, position, row):
    base = pl.multiple_of((position // TILE) * TILE, TILE)
    window = ref[lead + (pl.ds(base, TILE), slice(None))]
    at = lax.broadcasted_iota(jnp.int32, window.shape, 0) == position - base
    ref[lead + (pl.ds(base, TILE), slice(None))] = jnp.where(at, bcast_rows(row, TILE), window)


def find_leaver(targets_ref, source_inst, target_inst):
    slot = jnp.int32(0)
    place = jnp.int32(0)
    for j in range(REQS):
        t = targets_ref[source_inst * REQS + j]
        hit = t // REQS == target_inst
        slot = jnp.where(hit, j, slot)
        place = jnp.where(hit, t % REQS, place)
    return slot, place


def attend_kernel(shifts, groups, targets_hbm, lengths_hbm, queries_hbm, new_hbm, caches_hbm, *rest):
    lead_far, lead_near, tail_near, tail_far = rest[:4]
    (places, att, after_hbm, targets, lengths, queries, new, stored, query, small_sems, in_sems,
     out_sems) = rest[4:]
    me = lax.axis_index("inst")
    smalls = [
        pltpu.make_async_copy(source, target, small_sems.at[n])
        for n, (source, target) in enumerate(
            [(lengths_hbm, lengths), (new_hbm, new), (targets_hbm, targets), (queries_hbm, queries)]
        )
    ]

    def load(s, kv):
        return pltpu.make_async_copy(caches_hbm.at[kv, s], stored.at[kv, s], in_sems.at[kv, s])

    def save(s, kv):
        return pltpu.make_async_copy(stored.at[kv, s], after_hbm.at[kv, s], out_sems.at[kv, s])

    for copy in smalls:
        copy.start()
    for kv in range(2):
        for s in range(REQS):
            load(s, kv).start()
    for copy in smalls:
        copy.wait()
    slots = [find_leaver(targets, me, lax.rem(me + shift, groups))[0] for shift in shifts]
    for n, shift in enumerate(shifts):
        _, place = find_leaver(targets, lax.rem(me + groups - shift, groups), me)
        places[n:n + 1, :] = jnp.full((1, HD), place.astype(jnp.float32))
    for step in range(2):
        for h in range(8):
            rows = queries[step, :, h * HD:(h + 1) * HD].astype(jnp.float32)
            query[pl.ds(step * 8 + h, REQS, stride=16), :] = rows
    for kv in range(2):
        for s in range(REQS):
            load(s, kv).wait()
            for step in range(2):
                write_row(stored, (kv, s), lengths[me * REQS + s] + step, new[step, kv, s:s + 1, :])
            save(s, kv).start()
    probs = []
    for s in range(REQS):
        scores = lax.dot_general(
            query[s * 16:(s + 1) * 16, :].astype(BF), stored[0, s], (((1,), (1,)), ((), ())),
            preferred_element_type=jnp.float32,
        ) * HD ** (-0.5)
        live = lengths[me * REQS + s] + (
            lax.broadcasted_iota(jnp.int32, scores.shape, 0) >= 8
        ).astype(jnp.int32)
        visible = lax.broadcasted_iota(jnp.int32, scores.shape, 1) <= live
        scores = jnp.where(visible, scores, -jnp.inf)
        weights = jnp.exp(scores - jnp.max(scores, axis=-1, keepdims=True))
        probs.append((weights / jnp.sum(weights, axis=-1, keepdims=True)).astype(BF))
    for s in range(REQS):
        out = jnp.dot(probs[s], stored[1, s], preferred_element_type=jnp.float32)
        att[s * 8:(s + 1) * 8, :] = out[:8]
        att[(REQS + s) * 8:(REQS + s + 1) * 8, :] = out[8:]
    for shift, slot, lead in zip(shifts, slots, (lead_far, lead_near)):
        row = att[pl.ds(pl.multiple_of((REQS + slot) * 8, 8), 8), :]
        lead[:TILE, :] = jnp.concatenate([row, row], axis=0).astype(BF)
        if shift == 1:
            lead[TILE:TILE + CAP, :] = stored[0, slot]
            lead[TILE + CAP:, :] = stored[1, slot, :NEAR]
            tail_near[...] = stored[1, slot, NEAR:]
        else:
            for kv in range(2):
                lead[TILE + kv * FAR:TILE + (kv + 1) * FAR, :] = stored[kv, slot, :FAR]
                tail_far[kv * (CAP - FAR):(kv + 1) * (CAP - FAR), :] = stored[kv, slot, FAR:]
    for kv in range(2):
        for s in range(REQS):
            save(s, kv).wait()


def place_of(places_ref, n):
    return jnp.max(places_ref[n:n + 1, :]).astype(jnp.int32)


def project_kernel(parts, places_ref, att_ref, near_ref, far_ref, weight_ref, out_ref, att, lhs):
    width = out_ref.shape[-1]
    att[...] = att_ref[...]
    for n, pay in enumerate((far_ref, near_ref)):
        place = place_of(places_ref, n)
        att[pl.ds(pl.multiple_of((REQS + place) * 8, 8), 8), :] = pay[:TILE, :].astype(jnp.float32)[:8]
    for h in range(8):
        lhs[:, h * HD:(h + 1) * HD] = att[pl.ds(h, 2 * REQS, stride=8), :].astype(BF)
    for p in range(parts):
        out_ref[p] = jnp.dot(
            lhs[...], weight_ref[:, p * width:(p + 1) * width], preferred_element_type=jnp.float32
        ).astype(BF)


def start_placing(plan, places_ref, moved, after_hbm, sems):
    pairs = []
    for (n, pieces), source in zip(plan, moved):
        place = place_of(places_ref, n)
        for first, rows, kv, position in pieces:
            pairs.append((source.at[pl.ds(first, rows)], after_hbm.at[kv, place, pl.ds(position, rows)]))
    copies = [pltpu.make_async_copy(a, b, sems.at[n]) for n, (a, b) in enumerate(pairs)]
    for copy in copies:
        copy.start()
    return copies


def place_kernel(plan, places_ref, *rest):
    moved = rest[:len(plan)]
    _, after_hbm, sems = rest[len(plan):]
    for copy in start_placing(plan, places_ref, moved, after_hbm, sems):
        copy.wait()


def finish_kernel(plan, places_ref, *rest):
    moved = rest[:len(plan)]
    _, shares_ref, after_hbm, one_ref, two_ref, sems = rest[len(plan):]
    copies = start_placing(plan, places_ref, moved, after_hbm, sems)
    total = jnp.sum(shares_ref[...].astype(jnp.float32), axis=0)
    one_ref[...] = total[:REQS].astype(BF)
    two_ref[...] = total[REQS:].astype(BF)
    for copy in copies:
        copy.wait()


def pieces_of(first, rows, kv, position, cuts):
    step = rows // cuts
    return [(first + c * step, step, kv, position + c * step) for c in range(cuts)]


VM = pl.BlockSpec(memory_space=pltpu.VMEM)
HBM = pl.BlockSpec(memory_space=pltpu.HBM)
BF = jnp.bfloat16


def shape(dims, kind=BF):
    return jax.ShapeDtypeStruct(dims, kind)


def limit(mib):
    return pltpu.CompilerParams(vmem_limit_bytes=mib << 20)


def on_device(caches, queries, new_entries, lengths, targets, output_weight):
    groups = lax.axis_size("inst")
    parts = lax.axis_size("tp")
    shifts = (groups // 2, 1)
    many = len(shifts)
    width = output_weight.shape[1] // parts
    perms = [[(i, (i + s) % groups) for i in range(groups)] for s in shifts]

    caches, queries, new_entries, lengths, targets = [
        pltpu.with_memory_space_constraint(x, pltpu.HBM)
        for x in (caches, queries, new_entries, lengths, targets)
    ]
    *packs, places, att, after = pl.pallas_call(
        functools.partial(attend_kernel, shifts, groups),
        out_shape=[shape((TILE + 2 * FAR, HD)), shape((TILE + CAP + NEAR, HD)), shape((CAP - NEAR, HD)),
                   shape((2 * (CAP - FAR), HD))]
        + [shape((8, HD), jnp.float32), shape((16 * REQS, HD), jnp.float32), shape(caches.shape)],
        in_specs=[HBM] * 5,
        out_specs=[VM] * 6 + [HBM],
        scratch_shapes=[
            pltpu.SMEM(targets.shape, jnp.int32),
            pltpu.SMEM(lengths.shape, jnp.int32),
            pltpu.VMEM(queries.shape, BF),
            pltpu.VMEM(new_entries.shape, BF),
            pltpu.VMEM(caches.shape, BF),
            pltpu.VMEM((16 * REQS, HD), jnp.float32),
            pltpu.SemaphoreType.DMA((4,)),
            pltpu.SemaphoreType.DMA((2, REQS)),
            pltpu.SemaphoreType.DMA((2, REQS)),
        ],
        compiler_params=limit(6),
        cost_estimate=pl.CostEstimate(flops=10000000000, bytes_accessed=10**6, transcendentals=0),
        name="attend",
    )(targets, lengths, queries, new_entries, caches)
    lead_far, lead_near, tail_near, tail_far = [
        lax.ppermute(x, "inst", perms[n]) for x, n in zip(packs, (0, 1, 1, 0))
    ]

    partial = pl.pallas_call(
        functools.partial(project_kernel, parts),
        out_shape=shape((parts, 2 * REQS, width)),
        in_specs=[VM] * 5,
        out_specs=VM,
        scratch_shapes=[
            pltpu.VMEM((16 * REQS, HD), jnp.float32),
            pltpu.VMEM((2 * REQS, 8 * HD), BF),
        ],
        compiler_params=limit(20),
        cost_estimate=pl.CostEstimate(flops=1000000000, bytes_accessed=10**6, transcendentals=0),
        name="project",
    )(places, att, lead_near, lead_far, output_weight)
    shares = lax.all_to_all(partial, "tp", 0, 0)

    plan = [
        (1, pieces_of(TILE, CAP, 0, 0, 2) + pieces_of(TILE + CAP, NEAR, 1, 0, 1)),
        (0, [piece for kv in range(2) for piece in pieces_of(TILE + kv * FAR, FAR, kv, 0, 1)]),
    ]
    after = pl.pallas_call(
        functools.partial(place_kernel, plan),
        out_shape=shape(caches.shape),
        in_specs=[VM] * 3 + [HBM],
        out_specs=HBM,
        input_output_aliases={3: 0},
        scratch_shapes=[pltpu.SemaphoreType.DMA((sum(len(pieces) for _, pieces in plan),))],
        compiler_params=limit(4),
        cost_estimate=pl.CostEstimate(flops=2000000000, bytes_accessed=10**6, transcendentals=0),
        name="place",
    )(places, lead_near, lead_far, after)

    rest = CAP - FAR
    plan = [
        (1, pieces_of(0, CAP - NEAR, 1, NEAR, 1)),
        (0, [piece for kv in range(2) for piece in pieces_of(kv * rest, rest, kv, FAR, 2)]),
    ]
    after, one, two = pl.pallas_call(
        functools.partial(finish_kernel, plan),
        out_shape=[shape(caches.shape)] + [shape((REQS, width))] * 2,
        in_specs=[VM] * 3 + [HBM, VM],
        out_specs=[HBM, VM, VM],
        input_output_aliases={3: 0},
        scratch_shapes=[pltpu.SemaphoreType.DMA((sum(len(pieces) for _, pieces in plan),))],
        compiler_params=limit(4),
        name="finish",
    )(places, tail_near, tail_far, after, shares)
    return one, two, after


def solution(mesh):
    placed = (
        P(None, "inst", None, "tp"),
        P(None, "inst", "tp"),
        P(None, None, "inst", "tp"),
        P(),
        P(),
        P("tp", None),
    )
    return jax.shard_map(
        on_device,
        mesh=mesh,
        in_specs=placed,
        out_specs=(P("inst", "tp"), P("inst", "tp"), P(None, "inst", None, "tp")),
        check_vma=False,
    )
```

```python
import functools

import jax
import jax.numpy as jnp
from jax import lax
from jax.experimental import pallas as pl
from jax.experimental.pallas import tpu as pltpu
from jax.sharding import PartitionSpec as P

HD = 128
REQS = 4
CAP = 512
TILE = 16
FAR = 64
NEAR = 128


def bcast_rows(row, rows):
    return jnp.broadcast_to(row, (rows, row.shape[-1]))


def write_tokens(ref, kv, lengths, new):
    writes = []
    for s, length in enumerate(lengths):
        for position in (length, length + 1):
            base = pl.multiple_of((position // TILE) * TILE, TILE)
            window = ref[kv, s, pl.ds(base, TILE), :]
            row = lax.broadcasted_iota(jnp.int32, window.shape, 0) + base
            for step in range(2):
                window = jnp.where(row == length + step, bcast_rows(new[step, kv, s:s + 1, :], TILE), window)
            writes.append((s, base, window))
    for s, base, window in writes:
        ref[kv, s, pl.ds(base, TILE), :] = window


def find_leaver(targets_ref, source_inst, target_inst):
    slot = jnp.int32(0)
    place = jnp.int32(0)
    for j in range(REQS):
        t = targets_ref[source_inst * REQS + j]
        hit = t // REQS == target_inst
        slot = jnp.where(hit, j, slot)
        place = jnp.where(hit, t % REQS, place)
    return slot, place


def attend_kernel(shifts, groups, targets_hbm, lengths_hbm, queries_hbm, new_hbm, caches_hbm, *rest):
    lead_far, lead_near, tail_near, tail_far = rest[:4]
    places, att, stored, targets, lengths, queries, new, query, small_sems, in_sems = rest[4:]
    me = lax.axis_index("inst")
    smalls = [
        pltpu.make_async_copy(source, target, small_sems.at[n])
        for n, (source, target) in enumerate(
            [(lengths_hbm, lengths), (new_hbm, new), (targets_hbm, targets), (queries_hbm, queries)]
        )
    ]

    def load(s, kv):
        return pltpu.make_async_copy(caches_hbm.at[kv, s], stored.at[kv, s], in_sems.at[kv, s])

    for copy in smalls:
        copy.start()
    for kv in range(2):
        for s in range(REQS):
            load(s, kv).start()
    for copy in smalls:
        copy.wait()
    slots = [find_leaver(targets, me, lax.rem(me + shift, groups))[0] for shift in shifts]
    for n, shift in enumerate(shifts):
        _, place = find_leaver(targets, lax.rem(me + groups - shift, groups), me)
        places[n:n + 1, :] = jnp.full((1, HD), place.astype(jnp.float32))
    for step in range(2):
        for h in range(8):
            rows = queries[step, :, h * HD:(h + 1) * HD].astype(jnp.float32)
            query[pl.ds(step * 8 + h, REQS, stride=16), :] = rows
    own_lengths = [lengths[me * REQS + s] for s in range(REQS)]
    for kv in range(2):
        for s in range(REQS):
            load(s, kv).wait()
        write_tokens(stored, kv, own_lengths, new)
    probs = []
    for s in range(REQS):
        scores = lax.dot_general(
            query[s * 16:(s + 1) * 16, :].astype(BF), stored[0, s], (((1,), (1,)), ((), ())),
            preferred_element_type=jnp.float32,
        ) * HD ** (-0.5)
        live = own_lengths[s] + (
            lax.broadcasted_iota(jnp.int32, scores.shape, 0) >= 8
        ).astype(jnp.int32)
        visible = lax.broadcasted_iota(jnp.int32, scores.shape, 1) <= live
        scores = jnp.where(visible, scores, -jnp.inf)
        weights = jnp.exp(scores - jnp.max(scores, axis=-1, keepdims=True))
        probs.append((weights / jnp.sum(weights, axis=-1, keepdims=True)).astype(BF))
    for s in range(REQS):
        out = jnp.dot(probs[s], stored[1, s], preferred_element_type=jnp.float32)
        att[s * 8:(s + 1) * 8, :] = out[:8]
        att[(REQS + s) * 8:(REQS + s + 1) * 8, :] = out[8:]
    for shift, slot, lead in zip(shifts, slots, (lead_far, lead_near)):
        row = att[pl.ds(pl.multiple_of((REQS + slot) * 8, 8), 8), :]
        lead[:TILE, :] = jnp.concatenate([row, row], axis=0).astype(BF)
        if shift == 1:
            lead[TILE:TILE + CAP, :] = stored[0, slot]
            lead[TILE + CAP:, :] = stored[1, slot, :NEAR]
            tail_near[...] = stored[1, slot, NEAR:]
        else:
            for kv in range(2):
                lead[TILE + kv * FAR:TILE + (kv + 1) * FAR, :] = stored[kv, slot, :FAR]
                tail_far[kv * (CAP - FAR):(kv + 1) * (CAP - FAR), :] = stored[kv, slot, FAR:]


def place_of(places_ref, n):
    return jnp.max(places_ref[n:n + 1, :]).astype(jnp.int32)


def project_kernel(parts, places_ref, att_ref, near_ref, far_ref, weight_ref, out_ref, lhs):
    width = out_ref.shape[-1]
    rows = lax.broadcasted_iota(jnp.int32, (2 * REQS, HD), 0).astype(jnp.float32)
    pays = [pay[:TILE, :].astype(jnp.float32) for pay in (far_ref, near_ref)]
    for h in range(8):
        head = att_ref[pl.ds(h, 2 * REQS, stride=8), :]
        for n, pay in enumerate(pays):
            at = rows == bcast_rows(places_ref[n:n + 1, :] + REQS, 2 * REQS)
            head = jnp.where(at, bcast_rows(pay[h:h + 1], 2 * REQS), head)
        lhs[:, h * HD:(h + 1) * HD] = head.astype(BF)
    for p in range(0, parts, 2):
        both = jnp.dot(
            lhs[...], weight_ref[:, p * width:(p + 2) * width], preferred_element_type=jnp.float32
        ).astype(BF)
        out_ref[p] = both[:, :width]
        out_ref[p + 1] = both[:, width:]


def start_placing(plan, places_ref, moved, after_hbm, sems):
    pairs = []
    for (n, pieces), source in zip(plan, moved):
        place = place_of(places_ref, n)
        for first, rows, kv, position in pieces:
            pairs.append((source.at[pl.ds(first, rows)], after_hbm.at[kv, place, pl.ds(position, rows)]))
    copies = [pltpu.make_async_copy(a, b, sems.at[n]) for n, (a, b) in enumerate(pairs)]
    for copy in copies:
        copy.start()
    return copies


def place_kernel(plan, places_ref, near_ref, far_ref, stored, after_hbm, sems, stay_sems):
    copies = start_placing(plan, places_ref, (near_ref, far_ref), after_hbm, sems)
    taken = [place_of(places_ref, n) for n in range(2)]

    def for_staying(act):
        for s in range(REQS):
            @pl.when((taken[0] != s) & (taken[1] != s))
            def _():
                for kv in range(2):
                    act(pltpu.make_async_copy(stored.at[kv, s], after_hbm.at[kv, s], stay_sems.at[kv, s]))

    for_staying(lambda copy: copy.start())
    for copy in copies:
        copy.wait()
    for_staying(lambda copy: copy.wait())


def finish_kernel(plan, places_ref, *rest):
    moved = rest[:len(plan)]
    _, shares_ref, after_hbm, one_hbm, two_hbm, one, two, sems, out_sems = rest[len(plan):]
    copies = start_placing(plan, places_ref, moved, after_hbm, sems)
    total = jnp.sum(shares_ref[...].astype(jnp.float32), axis=0)
    one[...] = total[:REQS].astype(BF)
    two[...] = total[REQS:].astype(BF)
    for n, (source, target) in enumerate(((one, one_hbm), (two, two_hbm))):
        copies.append(pltpu.make_async_copy(source, target, out_sems.at[n]))
        copies[-1].start()
    for copy in copies:
        copy.wait()


def pieces_of(first, rows, kv, position, cuts):
    step = rows // cuts
    return [(first + c * step, step, kv, position + c * step) for c in range(cuts)]


VM = pl.BlockSpec(memory_space=pltpu.VMEM)
HBM = pl.BlockSpec(memory_space=pltpu.HBM)
BF = jnp.bfloat16


def shape(dims, kind=BF):
    return jax.ShapeDtypeStruct(dims, kind)


def limit(mib):
    return pltpu.CompilerParams(vmem_limit_bytes=mib << 20)


def on_device(caches, queries, new_entries, lengths, targets, output_weight):
    groups = lax.axis_size("inst")
    parts = lax.axis_size("tp")
    shifts = (groups // 2, 1)
    many = len(shifts)
    width = output_weight.shape[1] // parts
    perms = [[(i, (i + s) % groups) for i in range(groups)] for s in shifts]

    caches, queries, new_entries, lengths, targets = [
        pltpu.with_memory_space_constraint(x, pltpu.HBM)
        for x in (caches, queries, new_entries, lengths, targets)
    ]
    *packs, places, att, stored = pl.pallas_call(
        functools.partial(attend_kernel, shifts, groups),
        out_shape=[shape((TILE + 2 * FAR, HD)), shape((TILE + CAP + NEAR, HD)), shape((CAP - NEAR, HD)),
                   shape((2 * (CAP - FAR), HD))]
        + [shape((8, HD), jnp.float32), shape((16 * REQS, HD), jnp.float32), shape(caches.shape)],
        in_specs=[HBM] * 5,
        out_specs=[VM] * 7,
        scratch_shapes=[
            pltpu.SMEM(targets.shape, jnp.int32),
            pltpu.SMEM(lengths.shape, jnp.int32),
            pltpu.VMEM(queries.shape, BF),
            pltpu.VMEM(new_entries.shape, BF),
            pltpu.VMEM((16 * REQS, HD), jnp.float32),
            pltpu.SemaphoreType.DMA((4,)),
            pltpu.SemaphoreType.DMA((2, REQS)),
        ],
        compiler_params=limit(6),
        cost_estimate=pl.CostEstimate(flops=10000000000, bytes_accessed=10**6, transcendentals=0),
        name="attend",
    )(targets, lengths, queries, new_entries, caches)
    lead_far, lead_near, tail_near, tail_far = [
        lax.ppermute(x, "inst", perms[n]) for x, n in zip(packs, (0, 1, 1, 0))
    ]

    partial = pl.pallas_call(
        functools.partial(project_kernel, parts),
        out_shape=shape((parts, 2 * REQS, width)),
        in_specs=[VM] * 5,
        out_specs=VM,
        scratch_shapes=[
            pltpu.VMEM((2 * REQS, 8 * HD), BF),
        ],
        compiler_params=limit(20),
        cost_estimate=pl.CostEstimate(flops=1000000000, bytes_accessed=10**6, transcendentals=0),
        name="project",
    )(places, att, lead_near, lead_far, output_weight)
    shares = lax.all_to_all(partial, "tp", 0, 0)

    plan = [
        (1, pieces_of(TILE, CAP, 0, 0, 2) + pieces_of(TILE + CAP, NEAR, 1, 0, 1)),
        (0, [piece for kv in range(2) for piece in pieces_of(TILE + kv * FAR, FAR, kv, 0, 1)]),
    ]
    after = pl.pallas_call(
        functools.partial(place_kernel, plan),
        out_shape=shape(caches.shape),
        in_specs=[VM] * 4,
        out_specs=HBM,
        scratch_shapes=[
            pltpu.SemaphoreType.DMA((sum(len(pieces) for _, pieces in plan),)),
            pltpu.SemaphoreType.DMA((2, REQS)),
        ],
        compiler_params=limit(4),
        cost_estimate=pl.CostEstimate(flops=2000000000, bytes_accessed=10**6, transcendentals=0),
        name="place",
    )(places, lead_near, lead_far, stored)

    rest = CAP - FAR
    plan = [
        (1, pieces_of(0, CAP - NEAR, 1, NEAR, 1)),
        (0, [piece for kv in range(2) for piece in pieces_of(kv * rest, rest, kv, FAR, 2)]),
    ]
    after, one, two = pl.pallas_call(
        functools.partial(finish_kernel, plan),
        out_shape=[shape(caches.shape)] + [shape((REQS, width))] * 2,
        in_specs=[VM] * 3 + [HBM, VM],
        out_specs=[HBM] * 3,
        input_output_aliases={3: 0},
        scratch_shapes=[pltpu.VMEM((REQS, width), BF)] * 2 + [
            pltpu.SemaphoreType.DMA((sum(len(pieces) for _, pieces in plan),)),
            pltpu.SemaphoreType.DMA((2,)),
        ],
        compiler_params=limit(4),
        name="finish",
    )(places, tail_near, tail_far, after, shares)
    return one, two, after


def solution(mesh):
    placed = (
        P(None, "inst", None, "tp"),
        P(None, "inst", "tp"),
        P(None, None, "inst", "tp"),
        P(),
        P(),
        P("tp", None),
    )
    return jax.shard_map(
        on_device,
        mesh=mesh,
        in_specs=placed,
        out_specs=(P("inst", "tp"), P("inst", "tp"), P(None, "inst", None, "tp")),
        check_vma=False,
    )
```

```python
import functools

import jax
import jax.numpy as jnp
from jax import lax
from jax.experimental import pallas as pl
from jax.experimental.pallas import tpu as pltpu
from jax.sharding import PartitionSpec as P

HD = 128
REQS = 4
CAP = 512
TILE = 16
FAR = 64
NEAR = 128


def bcast_rows(row, rows):
    return jnp.broadcast_to(row, (rows, row.shape[-1]))


def write_tokens(ref, kv, lengths, new):
    writes = []
    for s, length in enumerate(lengths):
        for position in (length, length + 1):
            base = pl.multiple_of((position // TILE) * TILE, TILE)
            window = ref[kv, s, pl.ds(base, TILE), :]
            row = lax.broadcasted_iota(jnp.int32, window.shape, 0) + base
            for step in range(2):
                window = jnp.where(row == length + step, bcast_rows(new[step, kv, s:s + 1, :], TILE), window)
            writes.append((s, base, window))
    for s, base, window in writes:
        ref[kv, s, pl.ds(base, TILE), :] = window


def find_leaver(targets_ref, source_inst, target_inst):
    slot = jnp.int32(0)
    place = jnp.int32(0)
    for j in range(REQS):
        t = targets_ref[source_inst * REQS + j]
        hit = t // REQS == target_inst
        slot = jnp.where(hit, j, slot)
        place = jnp.where(hit, t % REQS, place)
    return slot, place


def attend_kernel(shifts, groups, targets_hbm, lengths_hbm, queries_hbm, new_hbm, caches_hbm, *rest):
    lead_far, lead_near, tail_near, tail_far = rest[:4]
    places, att, stored, targets, lengths, queries, new, query, small_sems, in_sems = rest[4:]
    me = lax.axis_index("inst")
    smalls = [
        pltpu.make_async_copy(source, target, small_sems.at[n])
        for n, (source, target) in enumerate(
            [(lengths_hbm, lengths), (new_hbm, new), (targets_hbm, targets), (queries_hbm, queries)]
        )
    ]

    def load(s, kv):
        return pltpu.make_async_copy(caches_hbm.at[kv, s], stored.at[kv, s], in_sems.at[kv, s])

    for copy in smalls:
        copy.start()
    for kv in range(2):
        for s in range(REQS):
            load(s, kv).start()
    for copy in smalls:
        copy.wait()
    slots = [find_leaver(targets, me, lax.rem(me + shift, groups))[0] for shift in shifts]
    for n, shift in enumerate(shifts):
        _, place = find_leaver(targets, lax.rem(me + groups - shift, groups), me)
        places[n:n + 1, :] = jnp.full((1, HD), place.astype(jnp.float32))
    for step in range(2):
        for h in range(8):
            rows = queries[step, :, h * HD:(h + 1) * HD].astype(jnp.float32)
            query[pl.ds(step * 8 + h, REQS, stride=16), :] = rows
    own_lengths = [lengths[me * REQS + s] for s in range(REQS)]
    for kv in range(2):
        for s in range(REQS):
            load(s, kv).wait()
        write_tokens(stored, kv, own_lengths, new)
    probs = []
    for s in range(REQS):
        scores = lax.dot_general(
            query[s * 16:(s + 1) * 16, :].astype(BF), stored[0, s], (((1,), (1,)), ((), ())),
            preferred_element_type=jnp.float32,
        ) * HD ** (-0.5)
        live = own_lengths[s] + (
            lax.broadcasted_iota(jnp.int32, scores.shape, 0) >= 8
        ).astype(jnp.int32)
        visible = lax.broadcasted_iota(jnp.int32, scores.shape, 1) <= live
        scores = jnp.where(visible, scores, -jnp.inf)
        weights = jnp.exp(scores - jnp.max(scores, axis=-1, keepdims=True))
        probs.append((weights.astype(BF), jnp.sum(weights, axis=-1, keepdims=True)))
    for s in range(REQS):
        out = jnp.dot(probs[s][0], stored[1, s], preferred_element_type=jnp.float32) / probs[s][1]
        att[s * 8:(s + 1) * 8, :] = out[:8]
        att[(REQS + s) * 8:(REQS + s + 1) * 8, :] = out[8:]
    for shift, slot, lead in zip(shifts, slots, (lead_far, lead_near)):
        row = att[pl.ds(pl.multiple_of((REQS + slot) * 8, 8), 8), :]
        lead[:TILE, :] = jnp.concatenate([row, row], axis=0).astype(BF)
        if shift == 1:
            lead[TILE:TILE + CAP, :] = stored[0, slot]
            lead[TILE + CAP:, :] = stored[1, slot, :NEAR]
            tail_near[...] = stored[1, slot, NEAR:]
        else:
            for kv in range(2):
                lead[TILE + kv * FAR:TILE + (kv + 1) * FAR, :] = stored[kv, slot, :FAR]
                tail_far[kv * (CAP - FAR):(kv + 1) * (CAP - FAR), :] = stored[kv, slot, FAR:]


def place_of(places_ref, n):
    return jnp.max(places_ref[n:n + 1, :]).astype(jnp.int32)


def project_kernel(parts, places_ref, att_ref, near_ref, far_ref, weight_ref, mine_ref, theirs_ref, lhs):
    width = mine_ref.shape[-1]
    even = lax.rem(lax.axis_index("tp"), 2) == 0
    rows = lax.broadcasted_iota(jnp.int32, (2 * REQS, HD), 0).astype(jnp.float32)
    pays = [pay[:TILE, :].astype(jnp.float32) for pay in (far_ref, near_ref)]
    for h in range(8):
        head = att_ref[pl.ds(h, 2 * REQS, stride=8), :]
        for n, pay in enumerate(pays):
            at = rows == bcast_rows(places_ref[n:n + 1, :] + REQS, 2 * REQS)
            head = jnp.where(at, bcast_rows(pay[h:h + 1], 2 * REQS), head)
        lhs[:, h * HD:(h + 1) * HD] = head.astype(BF)
    for x in range(parts // 2):
        both = jnp.dot(
            lhs[...], weight_ref[:, 2 * x * width:2 * (x + 1) * width], preferred_element_type=jnp.float32
        )
        first, second = both[:, :width], both[:, width:]
        mine_ref[x] = jnp.where(even, first, second)
        theirs_ref[x] = jnp.where(even, second, first).astype(BF)


def add_kernel(chips, mine_ref, theirs_ref, own_ref, *sends):
    x = lax.axis_index("tp") // 2
    own_ref[...] = mine_ref[x] + theirs_ref[x].astype(jnp.float32)
    for d, send in enumerate(sends):
        to = lax.rem(x + d + 1, chips)
        send[...] = (mine_ref[to] + theirs_ref[to].astype(jnp.float32)).astype(BF)


def start_placing(plan, places_ref, moved, after_hbm, sems):
    pairs = []
    for (n, pieces), source in zip(plan, moved):
        place = place_of(places_ref, n)
        for first, rows, kv, position in pieces:
            pairs.append((source.at[pl.ds(first, rows)], after_hbm.at[kv, place, pl.ds(position, rows)]))
    copies = [pltpu.make_async_copy(a, b, sems.at[n]) for n, (a, b) in enumerate(pairs)]
    for copy in copies:
        copy.start()
    return copies


def place_kernel(plan, places_ref, near_ref, far_ref, stored, after_hbm, sems, stay_sems):
    copies = start_placing(plan, places_ref, (near_ref, far_ref), after_hbm, sems)
    taken = [place_of(places_ref, n) for n in range(2)]

    def for_staying(act):
        for s in range(REQS):
            @pl.when((taken[0] != s) & (taken[1] != s))
            def _():
                for kv in range(2):
                    act(pltpu.make_async_copy(stored.at[kv, s], after_hbm.at[kv, s], stay_sems.at[kv, s]))

    for_staying(lambda copy: copy.start())
    for copy in copies:
        copy.wait()
    for_staying(lambda copy: copy.wait())


def finish_kernel(plan, places_ref, *rest):
    moved = rest[:len(plan)]
    _, own_ref, *shares, after_hbm, one_hbm, two_hbm, one, two, sems, out_sems = rest[len(plan):]
    copies = start_placing(plan, places_ref, moved, after_hbm, sems)
    total = own_ref[...]
    for share in shares:
        total = total + share[...].astype(jnp.float32)
    one[...] = total[:REQS].astype(BF)
    two[...] = total[REQS:].astype(BF)
    for n, (source, target) in enumerate(((one, one_hbm), (two, two_hbm))):
        copies.append(pltpu.make_async_copy(source, target, out_sems.at[n]))
        copies[-1].start()
    for copy in copies:
        copy.wait()


def pieces_of(first, rows, kv, position, cuts):
    step = rows // cuts
    return [(first + c * step, step, kv, position + c * step) for c in range(cuts)]


VM = pl.BlockSpec(memory_space=pltpu.VMEM)
HBM = pl.BlockSpec(memory_space=pltpu.HBM)
BF = jnp.bfloat16


def shape(dims, kind=BF):
    return jax.ShapeDtypeStruct(dims, kind)


def limit(mib):
    return pltpu.CompilerParams(vmem_limit_bytes=mib << 20)


def on_device(caches, queries, new_entries, lengths, targets, output_weight):
    groups = lax.axis_size("inst")
    parts = lax.axis_size("tp")
    shifts = (groups // 2, 1)
    many = len(shifts)
    width = output_weight.shape[1] // parts
    perms = [[(i, (i + s) % groups) for i in range(groups)] for s in shifts]

    caches, queries, new_entries, lengths, targets = [
        pltpu.with_memory_space_constraint(x, pltpu.HBM)
        for x in (caches, queries, new_entries, lengths, targets)
    ]
    *packs, places, att, stored = pl.pallas_call(
        functools.partial(attend_kernel, shifts, groups),
        out_shape=[shape((TILE + 2 * FAR, HD)), shape((TILE + CAP + NEAR, HD)), shape((CAP - NEAR, HD)),
                   shape((2 * (CAP - FAR), HD))]
        + [shape((8, HD), jnp.float32), shape((16 * REQS, HD), jnp.float32), shape(caches.shape)],
        in_specs=[HBM] * 5,
        out_specs=[VM] * 7,
        scratch_shapes=[
            pltpu.SMEM(targets.shape, jnp.int32),
            pltpu.SMEM(lengths.shape, jnp.int32),
            pltpu.VMEM(queries.shape, BF),
            pltpu.VMEM(new_entries.shape, BF),
            pltpu.VMEM((16 * REQS, HD), jnp.float32),
            pltpu.SemaphoreType.DMA((4,)),
            pltpu.SemaphoreType.DMA((2, REQS)),
        ],
        compiler_params=limit(6),
        cost_estimate=pl.CostEstimate(flops=10000000000, bytes_accessed=10**6, transcendentals=0),
        name="attend",
    )(targets, lengths, queries, new_entries, caches)
    lead_far, lead_near, tail_near, tail_far = [
        lax.ppermute(x, "inst", perms[n]) for x, n in zip(packs, (0, 1, 1, 0))
    ]

    chips = parts // 2
    mine, theirs = pl.pallas_call(
        functools.partial(project_kernel, parts),
        out_shape=[shape((chips, 2 * REQS, width), jnp.float32), shape((chips, 2 * REQS, width))],
        in_specs=[VM] * 5,
        out_specs=[VM] * 2,
        scratch_shapes=[
            pltpu.VMEM((2 * REQS, 8 * HD), BF),
        ],
        compiler_params=limit(20),
        cost_estimate=pl.CostEstimate(flops=4000000000, bytes_accessed=10**6, transcendentals=0),
        name="project",
    )(places, att, lead_near, lead_far, output_weight)
    theirs = lax.ppermute(theirs, "tp", [(i, i + 1 - 2 * (i % 2)) for i in range(parts)])
    own, *shares = pl.pallas_call(
        functools.partial(add_kernel, chips),
        out_shape=[shape((2 * REQS, width), jnp.float32)] + [shape((2 * REQS, width))] * (chips - 1),
        in_specs=[VM] * 2,
        out_specs=[VM] * chips,
        compiler_params=limit(4),
        name="add",
    )(mine, theirs)
    shares = [
        lax.ppermute(x, "tp", [(i, (i + 2 * (d + 1)) % parts) for i in range(parts)]) for d, x in enumerate(shares)
    ]

    plan = [
        (1, pieces_of(TILE, CAP, 0, 0, 2) + pieces_of(TILE + CAP, NEAR, 1, 0, 1)),
        (0, [piece for kv in range(2) for piece in pieces_of(TILE + kv * FAR, FAR, kv, 0, 1)]),
    ]
    after = pl.pallas_call(
        functools.partial(place_kernel, plan),
        out_shape=shape(caches.shape),
        in_specs=[VM] * 4,
        out_specs=HBM,
        scratch_shapes=[
            pltpu.SemaphoreType.DMA((sum(len(pieces) for _, pieces in plan),)),
            pltpu.SemaphoreType.DMA((2, REQS)),
        ],
        compiler_params=limit(4),
        cost_estimate=pl.CostEstimate(flops=500000000, bytes_accessed=10**6, transcendentals=0),
        name="place",
    )(places, lead_near, lead_far, stored)

    rest = CAP - FAR
    plan = [
        (1, pieces_of(0, CAP - NEAR, 1, NEAR, 1)),
        (0, [piece for kv in range(2) for piece in pieces_of(kv * rest, rest, kv, FAR, 2)]),
    ]
    after, one, two = pl.pallas_call(
        functools.partial(finish_kernel, plan),
        out_shape=[shape(caches.shape)] + [shape((REQS, width))] * 2,
        in_specs=[VM] * 3 + [HBM] + [VM] * chips,
        out_specs=[HBM] * 3,
        input_output_aliases={3: 0},
        scratch_shapes=[pltpu.VMEM((REQS, width), BF)] * 2 + [
            pltpu.SemaphoreType.DMA((sum(len(pieces) for _, pieces in plan),)),
            pltpu.SemaphoreType.DMA((2,)),
        ],
        compiler_params=limit(4),
        name="finish",
    )(places, tail_near, tail_far, after, own, *shares)
    return one, two, after


def solution(mesh):
    placed = (
        P(None, "inst", None, "tp"),
        P(None, "inst", "tp"),
        P(None, None, "inst", "tp"),
        P(),
        P(),
        P("tp", None),
    )
    return jax.shard_map(
        on_device,
        mesh=mesh,
        in_specs=placed,
        out_specs=(P("inst", "tp"), P("inst", "tp"), P(None, "inst", None, "tp")),
        check_vma=False,
    )
```

```python
import functools

import jax
import jax.numpy as jnp
from jax import lax
from jax.experimental import pallas as pl
from jax.experimental.pallas import tpu as pltpu
from jax.sharding import PartitionSpec as P

HD = 128
REQS = 4
CAP = 512
TILE = 16
FAR = 64
NEAR = 128


def bcast_rows(row, rows):
    return jnp.broadcast_to(row, (rows, row.shape[-1]))


def write_tokens(ref, kv, lengths, new):
    writes = []
    for s, length in enumerate(lengths):
        for position in (length, length + 1):
            base = pl.multiple_of((position // TILE) * TILE, TILE)
            window = ref[kv, s, pl.ds(base, TILE), :]
            row = lax.broadcasted_iota(jnp.int32, window.shape, 0) + base
            for step in range(2):
                window = jnp.where(row == length + step, bcast_rows(new[step, kv, s:s + 1, :], TILE), window)
            writes.append((s, base, window))
    for s, base, window in writes:
        ref[kv, s, pl.ds(base, TILE), :] = window


def find_leaver(targets_ref, source_inst, target_inst):
    slot = jnp.int32(0)
    place = jnp.int32(0)
    for j in range(REQS):
        t = targets_ref[source_inst * REQS + j]
        hit = t // REQS == target_inst
        slot = jnp.where(hit, j, slot)
        place = jnp.where(hit, t % REQS, place)
    return slot, place


def attend_kernel(shifts, groups, targets_hbm, lengths_hbm, queries_hbm, new_hbm, caches_hbm, *rest):
    lead_far, lead_near, tail_near, tail_far = rest[:4]
    places, att, stored, targets, lengths, queries, new, query, small_sems, in_sems = rest[4:]
    me = lax.axis_index("inst")
    smalls = [
        pltpu.make_async_copy(source, target, small_sems.at[n])
        for n, (source, target) in enumerate(
            [(lengths_hbm, lengths), (new_hbm, new), (targets_hbm, targets), (queries_hbm, queries)]
        )
    ]

    def load(s, kv):
        return pltpu.make_async_copy(caches_hbm.at[kv, s], stored.at[kv, s], in_sems.at[kv, s])

    for copy in smalls:
        copy.start()
    for kv in range(2):
        for s in range(REQS):
            load(s, kv).start()
    for copy in smalls:
        copy.wait()
    slots = [find_leaver(targets, me, lax.rem(me + shift, groups))[0] for shift in shifts]
    for n, shift in enumerate(shifts):
        _, place = find_leaver(targets, lax.rem(me + groups - shift, groups), me)
        places[n:n + 1, :] = jnp.full((1, HD), place.astype(jnp.float32))
    for step in range(2):
        for h in range(8):
            rows = queries[step, :, h * HD:(h + 1) * HD].astype(jnp.float32)
            query[pl.ds(step * 8 + h, REQS, stride=16), :] = rows
    own_lengths = [lengths[me * REQS + s] for s in range(REQS)]
    for kv in range(2):
        for s in range(REQS):
            load(s, kv).wait()
        write_tokens(stored, kv, own_lengths, new)
    probs = []
    for s in range(REQS):
        scores = lax.dot_general(
            query[s * 16:(s + 1) * 16, :].astype(BF), stored[0, s], (((1,), (1,)), ((), ())),
            preferred_element_type=jnp.float32,
        ) * HD ** (-0.5)
        live = own_lengths[s] + (
            lax.broadcasted_iota(jnp.int32, scores.shape, 0) >= 8
        ).astype(jnp.int32)
        visible = lax.broadcasted_iota(jnp.int32, scores.shape, 1) <= live
        scores = jnp.where(visible, scores, -jnp.inf)
        weights = jnp.exp(scores - jnp.max(scores, axis=-1, keepdims=True))
        probs.append((weights.astype(BF), jnp.sum(weights, axis=-1, keepdims=True)))
    for s in range(REQS):
        out = jnp.dot(probs[s][0], stored[1, s], preferred_element_type=jnp.float32) / probs[s][1]
        att[s * 8:(s + 1) * 8, :] = out[:8]
        att[(REQS + s) * 8:(REQS + s + 1) * 8, :] = out[8:]
    for shift, slot, lead in zip(shifts, slots, (lead_far, lead_near)):
        row = att[pl.ds(pl.multiple_of((REQS + slot) * 8, 8), 8), :]
        lead[:TILE, :] = jnp.concatenate([row, row], axis=0).astype(BF)
        if shift == 1:
            lead[TILE:TILE + CAP, :] = stored[0, slot]
            lead[TILE + CAP:, :] = stored[1, slot, :NEAR]
            tail_near[...] = stored[1, slot, NEAR:]
        else:
            for kv in range(2):
                lead[TILE + kv * FAR:TILE + (kv + 1) * FAR, :] = stored[kv, slot, :FAR]
                tail_far[kv * (CAP - FAR):(kv + 1) * (CAP - FAR), :] = stored[kv, slot, FAR:]


def place_of(places_ref, n):
    return jnp.max(places_ref[n:n + 1, :]).astype(jnp.int32)


def project_kernel(places_ref, att_ref, near_ref, far_ref, weight_ref, theirs_ref, lhs):
    rows = lax.broadcasted_iota(jnp.int32, (2 * REQS, HD), 0).astype(jnp.float32)
    pays = [pay[:TILE, :].astype(jnp.float32) for pay in (far_ref, near_ref)]
    for h in range(8):
        head = att_ref[pl.ds(h, 2 * REQS, stride=8), :]
        for n, pay in enumerate(pays):
            at = rows == bcast_rows(places_ref[n:n + 1, :] + REQS, 2 * REQS)
            head = jnp.where(at, bcast_rows(pay[h:h + 1], 2 * REQS), head)
        lhs[:, h * HD:(h + 1) * HD] = head.astype(BF)
    project_half(lhs, weight_ref, 1, theirs_ref)


def project_half(lhs, weight_ref, other, out_ref):
    width = out_ref.shape[-1]
    core = lax.rem(lax.axis_index("tp") + other, 2)
    for x in range(out_ref.shape[0]):
        first = pl.multiple_of((2 * x + core) * width, HD)
        out_ref[x] = jnp.dot(
            lhs[...], weight_ref[:, pl.ds(first, width)], preferred_element_type=jnp.float32
        ).astype(out_ref.dtype)


def own_kernel(lhs, weight_ref, mine_ref):
    project_half(lhs, weight_ref, 0, mine_ref)


def add_kernel(chips, mine_ref, theirs_ref, own_ref, *sends):
    x = lax.axis_index("tp") // 2
    own_ref[...] = mine_ref[x] + theirs_ref[x].astype(jnp.float32)
    for d, send in enumerate(sends):
        to = lax.rem(x + d + 1, chips)
        send[...] = (mine_ref[to] + theirs_ref[to].astype(jnp.float32)).astype(BF)


def start_placing(plan, places_ref, moved, after_hbm, sems):
    pairs = []
    for (n, pieces), source in zip(plan, moved):
        place = place_of(places_ref, n)
        for first, rows, kv, position in pieces:
            pairs.append((source.at[pl.ds(first, rows)], after_hbm.at[kv, place, pl.ds(position, rows)]))
    copies = [pltpu.make_async_copy(a, b, sems.at[n]) for n, (a, b) in enumerate(pairs)]
    for copy in copies:
        copy.start()
    return copies


def place_kernel(plan, places_ref, near_ref, far_ref, stored, after_hbm, sems, stay_sems):
    copies = start_placing(plan, places_ref, (near_ref, far_ref), after_hbm, sems)
    taken = [place_of(places_ref, n) for n in range(2)]

    def for_staying(act):
        for s in range(REQS):
            @pl.when((taken[0] != s) & (taken[1] != s))
            def _():
                for kv in range(2):
                    act(pltpu.make_async_copy(stored.at[kv, s], after_hbm.at[kv, s], stay_sems.at[kv, s]))

    for_staying(lambda copy: copy.start())
    for copy in copies:
        copy.wait()
    for_staying(lambda copy: copy.wait())


def finish_kernel(plan, places_ref, *rest):
    moved = rest[:len(plan)]
    _, own_ref, *shares, after_hbm, one_hbm, two_hbm, one, two, sems, out_sems = rest[len(plan):]
    copies = start_placing(plan, places_ref, moved, after_hbm, sems)
    total = own_ref[...]
    for share in shares:
        total = total + share[...].astype(jnp.float32)
    one[...] = total[:REQS].astype(BF)
    two[...] = total[REQS:].astype(BF)
    for n, (source, target) in enumerate(((one, one_hbm), (two, two_hbm))):
        copies.append(pltpu.make_async_copy(source, target, out_sems.at[n]))
        copies[-1].start()
    for copy in copies:
        copy.wait()


def pieces_of(first, rows, kv, position, cuts):
    step = rows // cuts
    return [(first + c * step, step, kv, position + c * step) for c in range(cuts)]


VM = pl.BlockSpec(memory_space=pltpu.VMEM)
HBM = pl.BlockSpec(memory_space=pltpu.HBM)
BF = jnp.bfloat16


def shape(dims, kind=BF):
    return jax.ShapeDtypeStruct(dims, kind)


def limit(mib):
    return pltpu.CompilerParams(vmem_limit_bytes=mib << 20)


def on_device(caches, queries, new_entries, lengths, targets, output_weight):
    groups = lax.axis_size("inst")
    parts = lax.axis_size("tp")
    shifts = (groups // 2, 1)
    many = len(shifts)
    width = output_weight.shape[1] // parts
    perms = [[(i, (i + s) % groups) for i in range(groups)] for s in shifts]

    caches, queries, new_entries, lengths, targets = [
        pltpu.with_memory_space_constraint(x, pltpu.HBM)
        for x in (caches, queries, new_entries, lengths, targets)
    ]
    *packs, places, att, stored = pl.pallas_call(
        functools.partial(attend_kernel, shifts, groups),
        out_shape=[shape((TILE + 2 * FAR, HD)), shape((TILE + CAP + NEAR, HD)), shape((CAP - NEAR, HD)),
                   shape((2 * (CAP - FAR), HD))]
        + [shape((8, HD), jnp.float32), shape((16 * REQS, HD), jnp.float32), shape(caches.shape)],
        in_specs=[HBM] * 5,
        out_specs=[VM] * 7,
        scratch_shapes=[
            pltpu.SMEM(targets.shape, jnp.int32),
            pltpu.SMEM(lengths.shape, jnp.int32),
            pltpu.VMEM(queries.shape, BF),
            pltpu.VMEM(new_entries.shape, BF),
            pltpu.VMEM((16 * REQS, HD), jnp.float32),
            pltpu.SemaphoreType.DMA((4,)),
            pltpu.SemaphoreType.DMA((2, REQS)),
        ],
        compiler_params=limit(6),
        cost_estimate=pl.CostEstimate(flops=10000000000, bytes_accessed=10**6, transcendentals=0),
        name="attend",
    )(targets, lengths, queries, new_entries, caches)
    lead_far, lead_near, tail_near, tail_far = [
        lax.ppermute(x, "inst", perms[n]) for x, n in zip(packs, (0, 1, 1, 0))
    ]

    chips = parts // 2
    theirs, lhs = pl.pallas_call(
        project_kernel,
        out_shape=[shape((chips, 2 * REQS, width)), shape((2 * REQS, 8 * HD))],
        in_specs=[VM] * 5,
        out_specs=[VM] * 2,
        compiler_params=limit(20),
        cost_estimate=pl.CostEstimate(flops=4000000000, bytes_accessed=10**6, transcendentals=0),
        name="project",
    )(places, att, lead_near, lead_far, output_weight)
    mine = pl.pallas_call(
        own_kernel,
        out_shape=shape((chips, 2 * REQS, width), jnp.float32),
        in_specs=[VM] * 2,
        out_specs=VM,
        compiler_params=limit(20),
        cost_estimate=pl.CostEstimate(flops=10**9, bytes_accessed=10**6, transcendentals=0),
        name="own",
    )(lhs, output_weight)
    theirs = lax.ppermute(theirs, "tp", [(i, i + 1 - 2 * (i % 2)) for i in range(parts)])
    own, *shares = pl.pallas_call(
        functools.partial(add_kernel, chips),
        out_shape=[shape((2 * REQS, width), jnp.float32)] + [shape((2 * REQS, width))] * (chips - 1),
        in_specs=[VM] * 2,
        out_specs=[VM] * chips,
        compiler_params=limit(4),
        name="add",
    )(mine, theirs)
    shares = [
        lax.ppermute(x, "tp", [(i, (i + 2 * (d + 1)) % parts) for i in range(parts)]) for d, x in enumerate(shares)
    ]

    plan = [
        (1, pieces_of(TILE, CAP, 0, 0, 2) + pieces_of(TILE + CAP, NEAR, 1, 0, 1)),
        (0, [piece for kv in range(2) for piece in pieces_of(TILE + kv * FAR, FAR, kv, 0, 1)]),
    ]
    after = pl.pallas_call(
        functools.partial(place_kernel, plan),
        out_shape=shape(caches.shape),
        in_specs=[VM] * 4,
        out_specs=HBM,
        scratch_shapes=[
            pltpu.SemaphoreType.DMA((sum(len(pieces) for _, pieces in plan),)),
            pltpu.SemaphoreType.DMA((2, REQS)),
        ],
        compiler_params=limit(4),
        cost_estimate=pl.CostEstimate(flops=500000000, bytes_accessed=10**6, transcendentals=0),
        name="place",
    )(places, lead_near, lead_far, stored)

    rest = CAP - FAR
    plan = [
        (1, pieces_of(0, CAP - NEAR, 1, NEAR, 1)),
        (0, [piece for kv in range(2) for piece in pieces_of(kv * rest, rest, kv, FAR, 2)]),
    ]
    after, one, two = pl.pallas_call(
        functools.partial(finish_kernel, plan),
        out_shape=[shape(caches.shape)] + [shape((REQS, width))] * 2,
        in_specs=[VM] * 3 + [HBM] + [VM] * chips,
        out_specs=[HBM] * 3,
        input_output_aliases={3: 0},
        scratch_shapes=[pltpu.VMEM((REQS, width), BF)] * 2 + [
            pltpu.SemaphoreType.DMA((sum(len(pieces) for _, pieces in plan),)),
            pltpu.SemaphoreType.DMA((2,)),
        ],
        compiler_params=limit(4),
        name="finish",
    )(places, tail_near, tail_far, after, own, *shares)
    return one, two, after


def solution(mesh):
    placed = (
        P(None, "inst", None, "tp"),
        P(None, "inst", "tp"),
        P(None, None, "inst", "tp"),
        P(),
        P(),
        P("tp", None),
    )
    return jax.shard_map(
        on_device,
        mesh=mesh,
        in_specs=placed,
        out_specs=(P("inst", "tp"), P("inst", "tp"), P(None, "inst", None, "tp")),
        check_vma=False,
    )
```

```python
import functools

import jax
import jax.numpy as jnp
from jax import lax
from jax.experimental import pallas as pl
from jax.experimental.pallas import tpu as pltpu
from jax.sharding import PartitionSpec as P

HD = 128
REQS = 4
CAP = 512
TILE = 16
FAR = 64
NEAR = 128


def bcast_rows(row, rows):
    return jnp.broadcast_to(row, (rows, row.shape[-1]))


def write_tokens(ref, kv, lengths, new):
    writes = []
    for s, length in enumerate(lengths):
        for position in (length, length + 1):
            base = pl.multiple_of((position // TILE) * TILE, TILE)
            window = ref[kv, s, pl.ds(base, TILE), :]
            row = lax.broadcasted_iota(jnp.int32, window.shape, 0) + base
            for step in range(2):
                window = jnp.where(row == length + step, bcast_rows(new[step, kv, s:s + 1, :], TILE), window)
            writes.append((s, base, window))
    for s, base, window in writes:
        ref[kv, s, pl.ds(base, TILE), :] = window


def find_leaver(targets_ref, source_inst, target_inst):
    slot = jnp.int32(0)
    place = jnp.int32(0)
    for j in range(REQS):
        t = targets_ref[source_inst * REQS + j]
        hit = t // REQS == target_inst
        slot = jnp.where(hit, j, slot)
        place = jnp.where(hit, t % REQS, place)
    return slot, place


def attend_kernel(shifts, groups, targets_hbm, lengths_hbm, queries_hbm, new_hbm, caches_hbm, *rest):
    lead_far, lead_near, tail_near, tail_far = rest[:4]
    places, att, stored, targets, lengths, queries, new, query, small_sems, in_sems = rest[4:]
    me = lax.axis_index("inst")
    smalls = [
        pltpu.make_async_copy(source, target, small_sems.at[n])
        for n, (source, target) in enumerate(
            [(lengths_hbm, lengths), (new_hbm, new), (targets_hbm, targets), (queries_hbm, queries)]
        )
    ]

    def load(s, kv):
        return pltpu.make_async_copy(caches_hbm.at[kv, s], stored.at[kv, s], in_sems.at[kv, s])

    for copy in smalls:
        copy.start()
    for kv in range(2):
        for s in range(REQS):
            load(s, kv).start()
    for copy in smalls:
        copy.wait()
    slots = [find_leaver(targets, me, lax.rem(me + shift, groups))[0] for shift in shifts]
    for n, shift in enumerate(shifts):
        _, place = find_leaver(targets, lax.rem(me + groups - shift, groups), me)
        places[n:n + 1, :] = jnp.full((1, HD), place.astype(jnp.float32))
    for step in range(2):
        for h in range(8):
            rows = queries[step, :, h * HD:(h + 1) * HD].astype(jnp.float32)
            query[pl.ds(step * 8 + h, REQS, stride=16), :] = rows
    own_lengths = [lengths[me * REQS + s] for s in range(REQS)]
    for kv in range(2):
        for s in range(REQS):
            load(s, kv).wait()
        write_tokens(stored, kv, own_lengths, new)
    probs = []
    for s in range(REQS):
        scores = lax.dot_general(
            query[s * 16:(s + 1) * 16, :].astype(BF), stored[0, s], (((1,), (1,)), ((), ())),
            preferred_element_type=jnp.float32,
        ) * HD ** (-0.5)
        live = own_lengths[s] + (
            lax.broadcasted_iota(jnp.int32, scores.shape, 0) >= 8
        ).astype(jnp.int32)
        visible = lax.broadcasted_iota(jnp.int32, scores.shape, 1) <= live
        scores = jnp.where(visible, scores, -jnp.inf)
        weights = jnp.exp(scores - jnp.max(scores, axis=-1, keepdims=True))
        probs.append((weights.astype(BF), jnp.sum(weights, axis=-1, keepdims=True)))
    for s in range(REQS):
        out = jnp.dot(probs[s][0], stored[1, s], preferred_element_type=jnp.float32) / probs[s][1]
        att[s * 8:(s + 1) * 8, :] = out[:8]
        att[(REQS + s) * 8:(REQS + s + 1) * 8, :] = out[8:]
    for shift, slot, lead in zip(shifts, slots, (lead_far, lead_near)):
        row = att[pl.ds(pl.multiple_of((REQS + slot) * 8, 8), 8), :]
        lead[:TILE, :] = jnp.concatenate([row, row], axis=0).astype(BF)
        if shift == 1:
            lead[TILE:TILE + CAP, :] = stored[0, slot]
            lead[TILE + CAP:, :] = stored[1, slot, :NEAR]
            tail_near[...] = stored[1, slot, NEAR:]
        else:
            for kv in range(2):
                lead[TILE + kv * FAR:TILE + (kv + 1) * FAR, :] = stored[kv, slot, :FAR]
                tail_far[kv * (CAP - FAR):(kv + 1) * (CAP - FAR), :] = stored[kv, slot, FAR:]


def place_of(places_ref, n):
    return places_ref[n, 0].astype(jnp.int32)


def project_kernel(places_ref, att_ref, near_ref, far_ref, weight_ref, theirs_ref, lhs):
    rows = lax.broadcasted_iota(jnp.int32, (2 * REQS, HD), 0).astype(jnp.float32)
    pays = [pay[:TILE, :].astype(jnp.float32) for pay in (far_ref, near_ref)]
    for h in range(8):
        head = att_ref[pl.ds(h, 2 * REQS, stride=8), :]
        for n, pay in enumerate(pays):
            at = rows == bcast_rows(places_ref[n:n + 1, :] + REQS, 2 * REQS)
            head = jnp.where(at, bcast_rows(pay[h:h + 1], 2 * REQS), head)
        lhs[:, h * HD:(h + 1) * HD] = head.astype(BF)
    project_half(lhs, weight_ref, 1, theirs_ref)


def project_half(lhs, weight_ref, other, out_ref):
    width = out_ref.shape[-1]
    core = lax.rem(lax.axis_index("tp") + other, 2)
    for x in range(out_ref.shape[0]):
        first = pl.multiple_of((2 * x + core) * width, HD)
        out_ref[x] = jnp.dot(
            lhs[...], weight_ref[:, pl.ds(first, width)], preferred_element_type=jnp.float32
        ).astype(out_ref.dtype)


def own_kernel(lhs, weight_ref, mine_ref):
    project_half(lhs, weight_ref, 0, mine_ref)


def add_kernel(chips, mine_ref, theirs_ref, own_ref, *sends):
    x = lax.axis_index("tp") // 2
    own_ref[...] = mine_ref[x] + theirs_ref[x].astype(jnp.float32)
    for d, send in enumerate(sends):
        to = lax.rem(x + d + 1, chips)
        send[...] = (mine_ref[to] + theirs_ref[to].astype(jnp.float32)).astype(BF)


def start_placing(plan, places_ref, moved, after_hbm, sems):
    pairs = []
    for (n, pieces), source in zip(plan, moved):
        place = place_of(places_ref, n)
        for first, rows, kv, position in pieces:
            pairs.append((source.at[pl.ds(first, rows)], after_hbm.at[kv, place, pl.ds(position, rows)]))
    copies = [pltpu.make_async_copy(a, b, sems.at[n]) for n, (a, b) in enumerate(pairs)]
    for copy in copies:
        copy.start()
    return copies


def place_kernel(plan, places_ref, near_ref, far_ref, stored, after_hbm, sems, stay_sems):
    copies = start_placing(plan, places_ref, (near_ref, far_ref), after_hbm, sems)
    taken = [place_of(places_ref, n) for n in range(2)]

    def for_staying(act):
        for s in range(REQS):
            @pl.when((taken[0] != s) & (taken[1] != s))
            def _():
                for kv in range(2):
                    act(pltpu.make_async_copy(stored.at[kv, s], after_hbm.at[kv, s], stay_sems.at[kv, s]))

    for_staying(lambda copy: copy.start())
    for copy in copies:
        copy.wait()
    for_staying(lambda copy: copy.wait())


def finish_kernel(plan, places_ref, *rest):
    moved = rest[:len(plan)]
    _, own_ref, *shares, after_hbm, one_hbm, two_hbm, one, two, sems, out_sems = rest[len(plan):]
    copies = start_placing(plan, places_ref, moved, after_hbm, sems)
    total = own_ref[...]
    for share in shares:
        total = total + share[...].astype(jnp.float32)
    one[...] = total[:REQS].astype(BF)
    two[...] = total[REQS:].astype(BF)
    for n, (source, target) in enumerate(((one, one_hbm), (two, two_hbm))):
        copies.append(pltpu.make_async_copy(source, target, out_sems.at[n]))
        copies[-1].start()
    for copy in copies:
        copy.wait()


def pieces_of(first, rows, kv, position, cuts):
    step = rows // cuts
    return [(first + c * step, step, kv, position + c * step) for c in range(cuts)]


VM = pl.BlockSpec(memory_space=pltpu.VMEM)
HBM = pl.BlockSpec(memory_space=pltpu.HBM)
BF = jnp.bfloat16


def shape(dims, kind=BF):
    return jax.ShapeDtypeStruct(dims, kind)


def limit(mib):
    return pltpu.CompilerParams(vmem_limit_bytes=mib << 20)


def on_device(caches, queries, new_entries, lengths, targets, output_weight):
    groups = lax.axis_size("inst")
    parts = lax.axis_size("tp")
    shifts = (groups // 2, 1)
    many = len(shifts)
    width = output_weight.shape[1] // parts
    perms = [[(i, (i + s) % groups) for i in range(groups)] for s in shifts]

    caches, queries, new_entries, lengths, targets = [
        pltpu.with_memory_space_constraint(x, pltpu.HBM)
        for x in (caches, queries, new_entries, lengths, targets)
    ]
    *packs, places, att, stored = pl.pallas_call(
        functools.partial(attend_kernel, shifts, groups),
        out_shape=[shape((TILE + 2 * FAR, HD)), shape((TILE + CAP + NEAR, HD)), shape((CAP - NEAR, HD)),
                   shape((2 * (CAP - FAR), HD))]
        + [shape((8, HD), jnp.float32), shape((16 * REQS, HD), jnp.float32), shape(caches.shape)],
        in_specs=[HBM] * 5,
        out_specs=[VM] * 7,
        scratch_shapes=[
            pltpu.SMEM(targets.shape, jnp.int32),
            pltpu.SMEM(lengths.shape, jnp.int32),
            pltpu.VMEM(queries.shape, BF),
            pltpu.VMEM(new_entries.shape, BF),
            pltpu.VMEM((16 * REQS, HD), jnp.float32),
            pltpu.SemaphoreType.DMA((4,)),
            pltpu.SemaphoreType.DMA((2, REQS)),
        ],
        compiler_params=limit(6),
        cost_estimate=pl.CostEstimate(flops=10000000000, bytes_accessed=10**6, transcendentals=0),
        name="attend",
    )(targets, lengths, queries, new_entries, caches)
    lead_far, lead_near, tail_near, tail_far = [
        lax.ppermute(x, "inst", perms[n]) for x, n in zip(packs, (0, 1, 1, 0))
    ]

    chips = parts // 2
    theirs, lhs = pl.pallas_call(
        project_kernel,
        out_shape=[shape((chips, 2 * REQS, width)), shape((2 * REQS, 8 * HD))],
        in_specs=[VM] * 5,
        out_specs=[VM] * 2,
        compiler_params=limit(20),
        cost_estimate=pl.CostEstimate(flops=4000000000, bytes_accessed=10**6, transcendentals=0),
        name="project",
    )(places, att, lead_near, lead_far, output_weight)
    mine = pl.pallas_call(
        own_kernel,
        out_shape=shape((chips, 2 * REQS, width), jnp.float32),
        in_specs=[VM] * 2,
        out_specs=VM,
        compiler_params=limit(20),
        cost_estimate=pl.CostEstimate(flops=10**9, bytes_accessed=10**6, transcendentals=0),
        name="own",
    )(lhs, output_weight)
    theirs = lax.ppermute(theirs, "tp", [(i, i + 1 - 2 * (i % 2)) for i in range(parts)])
    own, *shares = pl.pallas_call(
        functools.partial(add_kernel, chips),
        out_shape=[shape((2 * REQS, width), jnp.float32)] + [shape((2 * REQS, width))] * (chips - 1),
        in_specs=[VM] * 2,
        out_specs=[VM] * chips,
        compiler_params=limit(4),
        name="add",
    )(mine, theirs)
    shares = [
        lax.ppermute(x, "tp", [(i, (i + 2 * (d + 1)) % parts) for i in range(parts)]) for d, x in enumerate(shares)
    ]

    plan = [
        (1, pieces_of(TILE, CAP, 0, 0, 2) + pieces_of(TILE + CAP, NEAR, 1, 0, 1)),
        (0, [piece for kv in range(2) for piece in pieces_of(TILE + kv * FAR, FAR, kv, 0, 1)]),
    ]
    after = pl.pallas_call(
        functools.partial(place_kernel, plan),
        out_shape=shape(caches.shape),
        in_specs=[VM] * 4,
        out_specs=HBM,
        scratch_shapes=[
            pltpu.SemaphoreType.DMA((sum(len(pieces) for _, pieces in plan),)),
            pltpu.SemaphoreType.DMA((2, REQS)),
        ],
        compiler_params=limit(4),
        cost_estimate=pl.CostEstimate(flops=500000000, bytes_accessed=10**6, transcendentals=0),
        name="place",
    )(places, lead_near, lead_far, stored)

    rest = CAP - FAR
    plan = [
        (1, pieces_of(0, CAP - NEAR, 1, NEAR, 1)),
        (0, [piece for kv in range(2) for piece in pieces_of(kv * rest, rest, kv, FAR, 2)]),
    ]
    after, one, two = pl.pallas_call(
        functools.partial(finish_kernel, plan),
        out_shape=[shape(caches.shape)] + [shape((REQS, width))] * 2,
        in_specs=[VM] * 3 + [HBM] + [VM] * chips,
        out_specs=[HBM] * 3,
        input_output_aliases={3: 0},
        scratch_shapes=[pltpu.VMEM((REQS, width), BF)] * 2 + [
            pltpu.SemaphoreType.DMA((sum(len(pieces) for _, pieces in plan),)),
            pltpu.SemaphoreType.DMA((2,)),
        ],
        compiler_params=limit(4),
        name="finish",
    )(places, tail_near, tail_far, after, own, *shares)
    return one, two, after


def solution(mesh):
    placed = (
        P(None, "inst", None, "tp"),
        P(None, "inst", "tp"),
        P(None, None, "inst", "tp"),
        P(),
        P(),
        P("tp", None),
    )
    return jax.shard_map(
        on_device,
        mesh=mesh,
        in_specs=placed,
        out_specs=(P("inst", "tp"), P("inst", "tp"), P(None, "inst", None, "tp")),
        check_vma=False,
    )
```
